256 devices in a mesh: ep: 32 (over z, x), etp: 8 (over y, core).
Axes of the slice: x: 4, y: 4, z: 8, core: 2. Of those that a mesh axis runs over, the one named last changes fastest.
Arguments:
- tokens: bfloat16 [8192, 5120], P('ep', 'etp'), may hold values from -6 to 6
- routes: int32 [8192, 1], P('ep'), may hold values from 0 to 15; in each aligned block of 256 rows (0 to 255, 256 to 511, ...) at most 24 rows name the same one
- router_gate: bfloat16 [8192, 1], P('ep'), may hold values from 0.19921875 to 1
- w_gate: bfloat16 [5120, 65536], P(None, ('ep', 'etp')), may hold values from -0.078125 to 0.078125
- w_up: bfloat16 [5120, 65536], P(None, ('ep', 'etp')), may hold values from -0.078125 to 0.078125
- w_down: bfloat16 [65536, 5120], P(('ep', 'etp')), may hold values from -0.375 to 0.375
Outputs:
- moe_out: bfloat16 [8192, 5120], P('ep', 'etp')
The draws below stay inside these ranges and needn't reach their ends.
Inputs may be any that keep to these rules, and one draw needn't show every extreme that they name: `routes`: in the rows of one index of ep no expert is named more than 24 times, and in every draw some expert is named exactly 24 times by some index's rows; every expert is named by some token.
All inputs are finite; a program needn't handle non-finite values.
Results may differ from the reference program's by a relative error of at most 0.019.
Values may be sent and summed in bfloat16 or wider, within the bound.
A program may use at most 128 MiB of HBM per device.

```python
import math
import jax
import jax.numpy as jnp
import numpy as np
from jax import lax

D = 5120
FF = 4096
TOK_DEV = 256
TOKENS = 8192
EXPERTS = 16
CAP = 24
BLOCKS = 16
UNIT = 256
N_EP = 32


def strengthened(drawn, rng, source, target, blocks, factor):
    owner, partner = [(jnp.arange(drawn.shape[axis_at]) // (drawn.shape[axis_at] // blocks)).reshape([-1 if axis == axis_at else 1 for axis in range(drawn.ndim)]) for axis_at in (source, target)]
    chosen = jax.random.permutation(rng, blocks)[partner]
    strong = (owner == chosen) | (owner == (partner + blocks // 2) % blocks)
    return jnp.where(strong, factor * drawn, drawn)


def block_scale(own_key, extent, shards, low, top_value):
    def one(axis_at, blocks):
        steps = jax.random.uniform(jax.random.fold_in(jax.random.fold_in(own_key, 6), axis_at), (blocks,), jnp.float32, low / len(shards), top_value / len(shards))
        return jnp.repeat(jnp.exp(steps), extent[axis_at] // blocks).reshape((-1,) + (1,) * (len(extent) - axis_at - 1))

    loudness = one(*shards[0])
    for cut in shards[1:]:
        loudness = loudness * one(*cut)
    return loudness


def routed_block(rng, own, number, rows, count, top, most, lean):
    sequence = jax.random.permutation(rng, count)
    heavy_load, ordinary = shares(count, rows * top, most, lean, True), shares(count, rows * top, most, lean, False)
    places = jnp.arange(count)

    def named(lengths, offset_by):
        used = int((lengths > 0).sum())
        fixed = max(1, used // 4)
        passed = fixed + (places - fixed + offset_by * (used - fixed)) % max(1, count - fixed)
        return jnp.zeros((count,), jnp.int32).at[sequence[jnp.where(places < fixed, places, passed)]].set(jnp.asarray(lengths, jnp.int32))

    lengths = jnp.where(number % 4 == 0, named(heavy_load, number // 4), named(ordinary, number - number // 4 - 1))
    mixed = jax.random.permutation(jax.random.fold_in(own, 3), count)
    donor, taker = mixed[0:count // 2 * 2:2], mixed[1:count // 2 * 2:2]
    margin = jnp.minimum(lengths[donor] - 1, most - lengths[taker]) // 2
    margin = jnp.where((donor == sequence[0]) | (taker == sequence[0]) | (lengths[taker] == 0), 0, jnp.maximum(margin, 0))
    passed = jax.random.randint(jax.random.fold_in(own, 4), (count // 2,), 0, 1 << 20) % (margin + 1)
    lengths = lengths.at[donor].add(-passed).at[taker].add(passed)
    members = jnp.searchsorted(jnp.cumsum(lengths), jnp.arange(rows * top), side="right").astype(jnp.int32)
    table = members.reshape(top, rows).T
    table = table[jax.random.permutation(jax.random.fold_in(own, 1), rows)]
    offset_by = jax.random.randint(jax.random.fold_in(own, 2), (rows, 1), 0, top)
    return jnp.take_along_axis(table, (jnp.arange(top)[None, :] + offset_by) % top, axis=1)


def shares(number_of, total, most, slope, full):
    weights = [(1 << 20) // math.isqrt(grade ** slope) + 1 for grade in range(1, number_of + 1)]
    largest = most if full else min(most, max(-(-total // number_of), total * weights[0] // sum(weights)))
    least = 1 if total - largest >= number_of - 1 else 0
    counts, spare = [largest] + [least] * (number_of - 1), total - largest - least * (number_of - 1)
    while spare > 0:
        movable = [i for i in range(1, number_of) if counts[i] < largest] or [i for i in range(1, number_of) if counts[i] < most]
        mass, left = sum([weights[i] for i in movable]), spare
        for i in movable:
            more = min(most - counts[i], max(1, left * weights[i] // mass), spare)
            counts[i] = counts[i] + more
            spare = spare - more
    return np.array(counts)


def gaussian(rng, shape, scale, limit, split=(), kind=jnp.bfloat16):
    gain = block_scale(rng, shape, split, -0.22, 0.18) if split else 1.0
    drawn = jax.random.normal(rng, shape, jnp.float32) * scale * gain
    return jnp.minimum(jnp.maximum(drawn, -limit), limit).astype(kind)


def bell_draw_with(stream_key, extent, deviation, reach, split, heavy, kind=jnp.bfloat16):
    array = deviation * jax.random.normal(stream_key, extent, jnp.float32)
    if split:
        array = array * block_scale(stream_key, extent, split, -0.22, 0.18)
    return jnp.clip(strengthened(array, jax.random.fold_in(stream_key, 3), *heavy), -reach, reach).astype(kind)


def setup_inputs(seed: int = 0) -> dict:
    key_of = jax.random.split(jax.random.key(seed), 7)
    tokens = gaussian(key_of[0], (TOKENS, D), 1.0, 6.0, ((0, 32), (1, 8)))
    routes_keys = jax.random.split(jax.random.fold_in(key_of[1], 1), TOKENS // TOK_DEV)
    routes_turns = jax.random.permutation(jax.random.fold_in(key_of[1], 3), TOKENS // TOK_DEV)
    routes = jax.vmap(lambda own, number: routed_block(jax.random.fold_in(key_of[1], 2), own, number, TOK_DEV, EXPERTS, 1, CAP, 2))(routes_keys, routes_turns).reshape((TOKENS, 1))
    router_gate = jnp.clip(0.19921875 + 0.80078125 * jax.random.uniform(key_of[2], (TOKENS, 1), jnp.float32) ** block_scale(key_of[2], (TOKENS, 1), ((0, 32),), -0.2, 0.2), 0.19921875, 1.0).astype(jnp.bfloat16)
    w_gate = gaussian(key_of[3], (D, EXPERTS * FF), D ** -0.5, 0.078125, ((1, 256),))
    w_up = gaussian(key_of[4], (D, EXPERTS * FF), D ** -0.5, 0.078125, ((1, 256),))
    w_down = bell_draw_with(key_of[5], (EXPERTS * FF, D), FF ** -0.5, 0.375, ((0, 256),), (0, 1, 256, 6.0))
    return dict(tokens=tokens, routes=routes, router_gate=router_gate, w_gate=w_gate, w_up=w_up, w_down=w_down)


def reference(tokens, routes, router_gate, w_gate, w_up, w_down):
    expert_of = routes[:, 0].astype(jnp.int32)
    most_rows = N_EP * CAP

    def one_expert(expert):
        chosen = jnp.nonzero(expert_of == expert, size=most_rows, fill_value=0)[0].astype(jnp.int32)
        live_count = jnp.sum((expert_of == expert).astype(jnp.int32))
        is_live = (jnp.arange(most_rows, dtype=jnp.int32) < live_count).astype(jnp.float32)
        selected = tokens[chosen]
        gate_cols = lax.dynamic_slice_in_dim(w_gate, (expert * FF).astype(jnp.int32), FF, 1)
        up_cols = lax.dynamic_slice_in_dim(w_up, (expert * FF).astype(jnp.int32), FF, 1)
        down_rows = lax.dynamic_slice_in_dim(w_down, (expert * FF).astype(jnp.int32), FF, 0)
        gate_pre = jnp.dot(selected, gate_cols, preferred_element_type=jnp.float32)
        up_pre = jnp.dot(selected, up_cols, preferred_element_type=jnp.float32)
        hidden = (jax.nn.silu(gate_pre) * up_pre).astype(jnp.bfloat16)
        summed = jnp.zeros((most_rows, D), jnp.float32)
        for block in range(BLOCKS):
            partial_out = jnp.dot(hidden[:, block * UNIT:(block + 1) * UNIT],
                                  down_rows[block * UNIT:(block + 1) * UNIT],
                                  preferred_element_type=jnp.float32)
            summed = summed + lax.optimization_barrier(partial_out.astype(jnp.bfloat16)).astype(jnp.float32)
        return chosen, summed * is_live[:, None]

    all_chosen, all_out = lax.map(one_expert, jnp.arange(EXPERTS, dtype=jnp.int32))
    expert_out = jnp.zeros((TOKENS, D), jnp.float32)
    expert_out = expert_out.at[all_chosen.reshape(-1)].add(all_out.reshape(-1, D))
    return (expert_out * router_gate.astype(jnp.float32)).astype(jnp.bfloat16)
```

```python
import functools

import jax
import jax.numpy as jnp
from jax import lax
from jax.experimental import pallas as pl
from jax.experimental.pallas import tpu as pltpu
from jax.sharding import PartitionSpec as P

MESH = pl.DeviceIdType.MESH
F32 = jnp.float32
BF16 = jnp.bfloat16

CHUNKS = ((0, 1), (7, 2), (6, 3), (5, 4))
NC = len(CHUNKS)


def kernel(sizes, tokens, routes, gate, w_gate, w_up, w_down, out,
           w_gu, w_dn, slots, outgo, zrecv, cross, xs, acc, parts, crecv,
           ring2, ring2_in, ring_up, ring_up_in, ring_dn, ring_dn_in,
           own, xn_out, xn_in, fin, xc_in, rets, retr,
           w_sem, send_sem, recv_sem):
    nx, ny, nz, cap, feat = sizes
    half = 4 * cap
    ep = lax.axis_index("ep")
    etp = lax.axis_index("etp")
    z, x = ep // nx, ep % nx
    y, c = etp // 2, etp % 2

    def at(zz, xx, yy, cc):
        return {"ep": zz * nx + xx, "etp": yy * 2 + cc}

    y_up, y_dn = at(z, x, (y + 1) % ny, c), at(z, x, (y + ny - 1) % ny, c)
    core = at(z, x, y, 1 - c)
    x_near = at(z, x + 1 - 2 * (x % 2), y, c)
    x_cross = at(z, nx - 1 - x, y, c)

    barrier = pltpu.get_barrier_semaphore()
    peers = [y_up, y_dn, core, x_near, x_cross] + [
        at((z + j) % nz, x, y, c) for j in range(1, nz)
    ]
    for peer in peers:
        pl.semaphore_signal(barrier, inc=1, device_id=peer, device_id_type=MESH)

    loads = []
    for r in range(ny):
        for k in range(2):
            shard = (((y + r) % ny) * 2 + (c + k) % 2) * feat
            shard = pl.multiple_of(shard, 128)
            into = pl.ds(k * feat, feat)
            unit = w_gate.shape[1]
            loads.append((w_gate.at[pl.ds(shard, feat), :], w_gu.at[r, into, pl.ds(0, unit)]))
            loads.append((w_up.at[pl.ds(shard, feat), :], w_gu.at[r, into, pl.ds(unit, unit)]))
            loads.append((w_down.at[:, pl.ds(shard, feat)], w_dn.at[r, :, into]))
    loads = [pltpu.make_async_copy(a, b, w_sem.at[i]) for i, (a, b) in enumerate(loads)]
    for load in loads:
        load.start()

    rows = routes.shape[0]
    expert = routes[...]
    lane = lax.broadcasted_iota(jnp.int32, (rows, 128), 1)
    onehot = (expert == lane).astype(F32)
    before = lax.broadcasted_iota(jnp.int32, (rows, rows), 1) < lax.broadcasted_iota(
        jnp.int32, (rows, rows), 0
    )
    ranks = jnp.dot(before.astype(F32).astype(BF16), onehot.astype(BF16), preferred_element_type=F32)
    rank = jnp.sum(ranks * onehot, axis=1, keepdims=True).astype(jnp.int32)
    unit_of = (z + nz - (expert >> 1)) & (nz - 1)
    other = (expert & 1) != x // 2
    slot = unit_of * (2 * cap) + jnp.where(other, cap, 0) + rank
    place = lax.broadcasted_iota(jnp.int32, (rows, nz * 2 * cap), 1)
    slots[...] = (slot == place).astype(F32).astype(BF16)
    sent = lax.dot_general(
        slots[...], tokens[...], (((0,), (0,)), ((), ())), preferred_element_type=F32
    )
    outgo[...] = sent.astype(BF16).reshape(nz, 2 * cap, feat)

    started = []
    used = [0]

    def send(src, dst, device):
        i = used[0]
        used[0] += 1
        copy = pltpu.make_async_remote_copy(
            src_ref=src, dst_ref=dst, send_sem=send_sem.at[i], recv_sem=recv_sem.at[i],
            device_id=device, device_id_type=MESH,
        )
        copy.start()
        started.append(copy)
        return copy

    pl.semaphore_wait(barrier, len(peers))

    z_copy = {}
    for pair in CHUNKS:
        for j in pair:
            if j:
                z_copy[j] = send(outgo.at[j], zrecv.at[j], at((z + nz - j) % nz, x, y, c))

    MINE, THEIRS = pl.ds(0, feat), pl.ds(feat, feat)
    LOW, HIGH = pl.ds(0, half), pl.ds(half, half)
    copies = [dict() for _ in CHUNKS]

    def unit_block(j):
        if j:
            z_copy[j].wait_recv()
            return zrecv[j].astype(F32)
        return outgo[j].astype(F32)

    def d1(k):
        first, second = (unit_block(j) for j in CHUNKS[k])
        xs[k, 0, : half // 2, :feat] = jnp.concatenate([first[:cap], second[:cap]], axis=0).astype(BF16)
        cross[k] = jnp.concatenate([first[cap:], second[cap:]], axis=0).astype(BF16)
        copies[k]["cross"] = send(
            cross.at[k], xs.at[k, 0, pl.ds(half // 2, half // 2), MINE], x_cross
        )

    def d2(k):
        co = copies[k]
        co["cross"].wait_recv()
        mine = xs.at[k, 0, LOW, MINE]
        co["xn"] = send(mine, xs.at[k, 0, HIGH, MINE], x_near)
        co["up_low"] = send(mine, xs.at[k, 3, LOW, MINE], y_up)
        co["dn_low"] = send(mine, xs.at[k, 1, LOW, MINE], y_dn)
        co["c0_low"] = send(mine, xs.at[k, 0, LOW, THEIRS], core)

    def d3(k):
        co = copies[k]
        co["xn"].wait_recv()
        mine = xs.at[k, 0, HIGH, MINE]
        co["dn_high"] = send(mine, xs.at[k, 1, HIGH, MINE], y_dn)
        co["up_high"] = send(mine, xs.at[k, 3, HIGH, MINE], y_up)
        co["c0_high"] = send(mine, xs.at[k, 0, HIGH, THEIRS], core)

    def d4(k):
        co = copies[k]
        co["up_low"].wait_recv()
        co["f_up"] = send(xs.at[k, 3, LOW, MINE], xs.at[k, 2, LOW, MINE], y_up)
        co["dn_high"].wait_recv()
        co["f_dn"] = send(xs.at[k, 1, HIGH, MINE], xs.at[k, 2, HIGH, MINE], y_dn)
        co["dn_low"].wait_recv()
        co["up_high"].wait_recv()
        co["c1"] = send(xs.at[k, 1, :, MINE], xs.at[k, 1, :, THEIRS], core)
        co["c3"] = send(xs.at[k, 3, :, MINE], xs.at[k, 3, :, THEIRS], core)

    def d5(k):
        co = copies[k]
        co["f_up"].wait_recv()
        co["f_dn"].wait_recv()
        co["c2"] = send(xs.at[k, 2, :, MINE], xs.at[k, 2, :, THEIRS], core)

    def compute(k):
        co = copies[k]
        if k == 0:
            for load in loads:
                load.wait()
        co["c0_low"].wait_recv()
        co["c0_high"].wait_recv()
        acc[...] = jnp.dot(xs[k, 0], w_gu[0], preferred_element_type=F32)
        co["c1"].wait_recv()
        acc[...] += jnp.dot(xs[k, 1], w_gu[1], preferred_element_type=F32)
        co["c3"].wait_recv()
        acc[...] += jnp.dot(xs[k, 3], w_gu[3], preferred_element_type=F32)
        co["c2"].wait_recv()
        acc[...] += jnp.dot(xs[k, 2], w_gu[2], preferred_element_type=F32)
        unit = w_gate.shape[1]
        pre = acc[:, :unit]
        hidden = (pre / (1.0 + jnp.exp(-pre)) * acc[:, unit:]).astype(BF16)
        for r in (2, 1, 3, 0):
            parts[k, r] = jnp.dot(hidden, w_dn[r], preferred_element_type=F32).astype(BF16)
            co["p", r] = send(parts.at[k, r, :, THEIRS], crecv.at[k, r], core)

    def chip_sum(k, r, rows):
        return parts[k, r, rows, :feat].astype(F32) + crecv[k, r, rows].astype(F32)

    ALL = pl.ds(0, 2 * half)

    def r1(k):
        co = copies[k]
        co["p", 2].wait_recv()
        ring2[k] = chip_sum(k, 2, ALL).astype(BF16)
        co["g_up"] = send(ring2.at[k, LOW], ring2_in.at[k, LOW], y_up)
        co["g_dn"] = send(ring2.at[k, HIGH], ring2_in.at[k, HIGH], y_dn)
        co["p", 1].wait_recv()
        ring_up[k, half:] = chip_sum(k, 1, HIGH).astype(BF16)
        co["s_up_high"] = send(ring_up.at[k, HIGH], ring_up_in.at[k, HIGH], y_up)
        co["p", 3].wait_recv()
        ring_dn[k, :half] = chip_sum(k, 3, LOW).astype(BF16)
        co["s_dn_low"] = send(ring_dn.at[k, LOW], ring_dn_in.at[k, LOW], y_dn)

    def r2(k):
        co = copies[k]
        co["g_up"].wait_recv()
        ring_up[k, :half] = (chip_sum(k, 1, LOW) + ring2_in[k, :half].astype(F32)).astype(BF16)
        co["s_up_low"] = send(ring_up.at[k, LOW], ring_up_in.at[k, LOW], y_up)
        co["g_dn"].wait_recv()
        ring_dn[k, half:] = (chip_sum(k, 3, HIGH) + ring2_in[k, half:].astype(F32)).astype(BF16)
        co["s_dn_high"] = send(ring_dn.at[k, HIGH], ring_dn_in.at[k, HIGH], y_dn)

    def ring_sum(k, rows):
        return chip_sum(k, 0, rows) + (
            ring_up_in[k, rows].astype(F32) + ring_dn_in[k, rows].astype(F32)
        )

    def r3(k):
        co = copies[k]
        co["p", 0].wait_recv()
        co["s_up_high"].wait_recv()
        co["s_dn_high"].wait_recv()
        xn_out[k] = ring_sum(k, HIGH).astype(BF16)
        co["xn_back"] = send(xn_out.at[k], xn_in.at[k], x_near)
        co["s_up_low"].wait_recv()
        co["s_dn_low"].wait_recv()
        own[k] = ring_sum(k, LOW)

    def r4(k):
        co = copies[k]
        co["xn_back"].wait_recv()
        fin[k] = (own[k] + xn_in[k].astype(F32)).astype(BF16)
        co["xc_back"] = send(fin.at[k, pl.ds(half // 2, half // 2)], xc_in.at[k], x_cross)

    def r5(k):
        copies[k]["xc_back"].wait_recv()
        kept = fin[k, : half // 2].astype(F32)
        crossed = xc_in[k].astype(F32)
        for i, j in enumerate(CHUNKS[k]):
            lo, hi = i * cap, (i + 1) * cap
            block = jnp.concatenate([kept[lo:hi], crossed[lo:hi]], axis=0).astype(BF16)
            if j:
                rets[j] = block
                z_back[j] = send(rets.at[j], retr.at[j], at((z + j) % nz, x, y, c))
            else:
                retr[j] = block

    z_back = {}
    ORDER = (
        (d1, 0), (d2, 0), (d1, 1), (d3, 0), (d2, 1), (d1, 2), (d4, 0), (d3, 1), (d2, 2),
        (d1, 3), (d5, 0), (d3, 2), (d2, 3), (d4, 1), (d3, 3), (compute, 0),
        (r1, 0), (d5, 1), (d4, 2), (compute, 1), (r2, 0), (r1, 1), (d5, 2), (d4, 3),
        (r3, 0), (compute, 2), (r2, 1), (r1, 2), (d5, 3), (r4, 0), (r3, 1), (r5, 0),
        (compute, 3), (r2, 2), (r1, 3), (r4, 1), (r3, 2), (r5, 1), (r2, 3), (r4, 2),
        (r5, 2), (r3, 3), (r4, 3), (r5, 3),
    )
    for stage, k in ORDER:
        stage(k)

    for j in range(1, nz):
        z_back[j].wait_recv()
    back = retr[...].reshape(nz * 2 * cap, feat)
    merged = jnp.dot(slots[...], back, preferred_element_type=F32)
    out[...] = (merged * gate[...].astype(F32)).astype(BF16)
    for copy in started:
        copy.wait_send()


def on_device(nx, ny, nz, tokens, routes, router_gate, w_gate, w_up, w_down):
    rows, feat = tokens.shape
    unit = w_gate.shape[1]
    cap = 3 * rows // (nx * nz)
    half = 4 * cap
    vm = pltpu.VMEM
    scratch = [
        vm((ny, 2 * feat, 2 * unit), BF16),
        vm((ny, unit, 2 * feat), BF16),
        vm((rows, nz * 2 * cap), BF16),
        vm((nz, 2 * cap, feat), BF16),
        vm((nz, 2 * cap, feat), BF16),
        vm((NC, half // 2, feat), BF16),
        vm((NC, ny, 2 * half, 2 * feat), BF16),
        vm((2 * half, 2 * unit), F32),
        vm((NC, ny, 2 * half, 2 * feat), BF16),
        vm((NC, ny, 2 * half, feat), BF16),
    ]
    scratch += [vm((NC, 2 * half, feat), BF16)] * 6
    scratch += [
        vm((NC, half, feat), F32),
        vm((NC, half, feat), BF16),
        vm((NC, half, feat), BF16),
        vm((NC, half, feat), BF16),
        vm((NC, half // 2, feat), BF16),
        vm((nz, 2 * cap, feat), BF16),
        vm((nz, 2 * cap, feat), BF16),
        pltpu.SemaphoreType.DMA((6 * ny,)),
        pltpu.SemaphoreType.DMA((26 * NC + 14,)),
        pltpu.SemaphoreType.DMA((26 * NC + 14,)),
    ]
    in_vmem = pl.BlockSpec(memory_space=pltpu.VMEM)
    in_hbm = pl.BlockSpec(memory_space=pl.ANY)
    return pl.pallas_call(
        functools.partial(kernel, (nx, ny, nz, cap, feat)),
        out_shape=jax.ShapeDtypeStruct((rows, feat), BF16),
        in_specs=[in_vmem] * 3 + [in_hbm] * 3,
        out_specs=in_vmem,
        scratch_shapes=scratch,
        compiler_params=pltpu.CompilerParams(
            collective_id=0, has_side_effects=True, vmem_limit_bytes=60 * 1024 * 1024
        ),
    )(tokens, routes, router_gate, w_gate, w_up, w_down)


def solution(mesh):
    nx, ny = 4, mesh.shape["etp"] // 2
    nz = mesh.shape["ep"] // nx
    return jax.shard_map(
        functools.partial(on_device, nx, ny, nz),
        mesh=mesh,
        in_specs=(
            P("ep", "etp"),
            P("ep", None),
            P("ep", None),
            P(None, ("ep", "etp")),
            P(None, ("ep", "etp")),
            P(("ep", "etp"), None),
        ),
        out_specs=P("ep", "etp"),
        check_vma=False,
    )
```

```python
import functools

import jax
import jax.numpy as jnp
from jax import lax
from jax.experimental import pallas as pl
from jax.experimental.pallas import tpu as pltpu
from jax.sharding import PartitionSpec as P

MESH = pl.DeviceIdType.MESH
F32 = jnp.float32
BF16 = jnp.bfloat16

CHUNKS = ((0, 1), (7, 2), (6, 3), (5, 4))
NC = len(CHUNKS)
WIDE_IN = (False, False, False, False)
WIDE_OUT = (False, False, False, False)

ORDER = (
    ("d1", 0), ("d2", 0), ("d1", 1), ("d3", 0), ("d4u", 0), ("d4d", 0), ("d6", 0, 0), ("d2", 1),
    ("d3", 1), ("d1", 2), ("d4a", 0), ("d6", 0, 3), ("d4d", 1), ("d6", 0, 1), ("d1", 3), ("d2", 2),
    ("d6", 1, 0), ("d4u", 1), ("d3", 2), ("d2", 3), ("d4a", 1), ("d5", 0), ("d6", 1, 1), ("d3", 3),
    ("d6", 2, 0), ("d4u", 2), ("d6", 1, 3), ("d4d", 2), ("d6", 3, 0), ("d4u", 3), ("d4a", 2),
    ("d6", 0, 2), ("d5", 1), ("d4d", 3), ("d6", 2, 3), ("c", 0), ("e", 0, 2), ("sC1", 0),
    ("e", 0, 1), ("d4a", 3), ("e", 0, 3), ("gC", 0), ("d5", 2), ("e", 0, 0), ("d6", 1, 2),
    ("d6", 2, 1), ("d6", 3, 3), ("c", 1), ("d5", 3), ("e", 1, 1), ("e", 1, 2), ("sC1", 1),
    ("e", 1, 3), ("sC2", 0), ("e", 1, 0), ("gAB", 0), ("gC", 1), ("d6", 3, 1), ("sAB1", 0),
    ("d6", 2, 2), ("c", 2), ("e", 2, 2), ("sC1", 2), ("e", 2, 1), ("sAB2", 0), ("e", 2, 3),
    ("e", 2, 0), ("sC2", 1), ("gC", 2), ("d6", 3, 2), ("rC", 0), ("sAB1", 1), ("gAB", 1), ("c", 3),
    ("e", 3, 2), ("e", 3, 1), ("sC2", 2), ("sC1", 3), ("e", 3, 3), ("rAB", 0), ("e", 3, 0),
    ("gAB", 2), ("gC", 3), ("sAB2", 1), ("rC", 1), ("rC", 2), ("sAB1", 2), ("r4", 0), ("r5", 0),
    ("sAB2", 2), ("rAB", 1), ("gAB", 3), ("sC2", 3), ("sAB1", 3), ("rAB", 2), ("sAB2", 3),
    ("rC", 3), ("r4", 1), ("r5", 1), ("r4", 2), ("r5", 2), ("rAB", 3), ("r4", 3), ("r5", 3),
)


def kernel(sizes, tokens, routes, gate, w_gate, w_up, w_down, out,
           w_gu, w_dn, slots, outgo, zrecv, cross, xs, acc, parts, crecv, xb_out, xb_in,
           ring2, ring2_in, ring_up, ring_up_in, ring_dn, ring_dn_in,
           own, xn_out, xn_in, fin, fin_x, xc_in, rets, retr,
           w_sem, send_sem, recv_sem):
    nx, ny, nz, cap, feat = sizes
    half, piece = 4 * cap, 2 * cap
    ep = lax.axis_index("ep")
    etp = lax.axis_index("etp")
    z, x = ep // nx, ep % nx
    y, c = etp // 2, etp % 2

    def at(zz, xx, yy, cc):
        return {"ep": zz * nx + xx, "etp": yy * 2 + cc}

    y_up, y_dn = at(z, x, (y + 1) % ny, c), at(z, x, (y + ny - 1) % ny, c)
    core = at(z, x, y, 1 - c)
    x_near = at(z, x + 1 - 2 * (x % 2), y, c)
    x_cross = at(z, nx - 1 - x, y, c)

    barrier = pltpu.get_barrier_semaphore()
    peers = [y_up, y_dn, core, x_near, x_cross] + [
        at((z + j) % nz, x, y, c) for j in range(1, nz)
    ]
    for peer in peers:
        pl.semaphore_signal(barrier, inc=1, device_id=peer, device_id_type=MESH)

    loads = []
    for r in range(ny):
        for k in range(2):
            shard = (((y + r) % ny) * 2 + (c + k) % 2) * feat
            shard = pl.multiple_of(shard, 128)
            into = pl.ds(k * feat, feat)
            unit = w_gate.shape[1]
            loads.append((w_gate.at[pl.ds(shard, feat), :], w_gu.at[r, into, pl.ds(0, unit)]))
            loads.append((w_up.at[pl.ds(shard, feat), :], w_gu.at[r, into, pl.ds(unit, unit)]))
            loads.append((w_down.at[:, pl.ds(shard, feat)], w_dn.at[r, :, into]))
    loads = [pltpu.make_async_copy(a, b, w_sem.at[i]) for i, (a, b) in enumerate(loads)]
    for load in loads:
        load.start()

    rows = routes.shape[1]
    expert = routes[...]
    onehot = (expert == lax.broadcasted_iota(jnp.int32, (nz * nx // 2, rows), 0)).astype(F32)
    before = lax.broadcasted_iota(jnp.int32, (rows, rows), 0) < lax.broadcasted_iota(
        jnp.int32, (rows, rows), 1
    )
    ranks = jnp.dot(onehot.astype(BF16), before.astype(F32).astype(BF16), preferred_element_type=F32)
    rank = jnp.sum(ranks * onehot, axis=0, keepdims=True).astype(jnp.int32)
    unit_of = (z + nz - (expert >> 1)) & (nz - 1)
    other = (expert & 1) != x // 2
    slot = unit_of * (2 * cap) + jnp.where(other, cap, 0) + rank
    place = lax.broadcasted_iota(jnp.int32, (nz * 2 * cap, rows), 0)
    chosen = (slot == place).astype(F32)
    sent = jnp.dot(chosen.astype(BF16), tokens[...], preferred_element_type=F32)
    outgo[...] = sent.astype(BF16).reshape(nz, 2 * cap, feat)
    slots[...] = (chosen * gate[...].astype(F32)).astype(BF16)

    started = []
    used = [0]

    def send(src, dst, device):
        i = used[0]
        used[0] += 1
        copy = pltpu.make_async_remote_copy(
            src_ref=src, dst_ref=dst, send_sem=send_sem.at[i], recv_sem=recv_sem.at[i],
            device_id=device, device_id_type=MESH,
        )
        copy.start()
        started.append(copy)
        return copy

    pl.semaphore_wait(barrier, len(peers))

    z_copy = {}
    for pair in CHUNKS:
        for j in pair:
            if j:
                z_copy[j] = send(outgo.at[j], zrecv.at[j], at((z + nz - j) % nz, x, y, c))

    MINE, THEIRS = pl.ds(0, feat), pl.ds(feat, feat)
    A, B, AB = pl.ds(0, piece), pl.ds(piece, piece), pl.ds(0, half)
    NEAR_A, NEAR_B, NEAR = pl.ds(half, piece), pl.ds(half + piece, piece), pl.ds(half, half)
    copies = [dict() for _ in CHUNKS]

    def wait(k, *names):
        for name in names:
            copy = copies[k][name]
            if copy is not None:
                copy.wait_recv()
                copies[k][name] = None

    def unit_block(j):
        if j:
            z_copy[j].wait_recv()
            return zrecv[j].astype(F32)
        return outgo[j].astype(F32)

    def d1(k):
        co = copies[k]
        first, second = (unit_block(j) for j in CHUNKS[k])
        cross[k] = jnp.concatenate([first[cap:], second[cap:]], axis=0).astype(BF16)
        co["cross"] = send(cross.at[k], xs.at[k, 0, B, MINE], x_cross)
        xs[k, 0, :piece, :feat] = jnp.concatenate([first[:cap], second[:cap]], axis=0).astype(BF16)
        mine = xs.at[k, 0, A, MINE]
        co["xnA"] = send(mine, xs.at[k, 0, NEAR_A, MINE], x_near)
        co["upA"] = send(mine, xs.at[k, 3, A, MINE], y_up)
        co["dnA"] = send(mine, xs.at[k, 1, A, MINE], y_dn)

    def near_b(k, r):
        copies[k]["xnB", r] = send(xs.at[k, r, B, MINE], xs.at[k, r, NEAR_B, MINE], x_near)

    def d2(k):
        co = copies[k]
        wait(k, "cross")
        near_b(k, 0)
        mine = xs.at[k, 0, B, MINE]
        co["upB"] = send(mine, xs.at[k, 3, B, MINE], y_up)
        co["dnB"] = send(mine, xs.at[k, 1, B, MINE], y_dn)
        co["c0"] = send(xs.at[k, 0, AB, MINE], xs.at[k, 0, AB, THEIRS], core)

    def d3(k):
        co = copies[k]
        wait(k, "xnA")
        if WIDE_IN[k]:
            wait(k, ("xnB", 0))
        rows_c = NEAR if WIDE_IN[k] else NEAR_A
        mine = xs.at[k, 0, rows_c, MINE]
        co["upC"] = send(mine, xs.at[k, 3, rows_c, MINE], y_up)
        co["dnC"] = send(mine, xs.at[k, 1, rows_c, MINE], y_dn)
        co["c0C"] = send(mine, xs.at[k, 0, rows_c, THEIRS], core)

    def pass_on(k, r, rows_of):
        src, device = ((3, y_up) if r > 0 else (1, y_dn))
        return send(xs.at[k, src, rows_of, MINE], xs.at[k, 2, rows_of, MINE], device)

    def d4u(k):
        wait(k, "upA", "upB")
        if not WIDE_IN[k]:
            near_b(k, 3)
        if k % 2 == 0:
            copies[k]["fAB"] = pass_on(k, 1, AB)

    def d4d(k):
        wait(k, "dnA", "dnB")
        if not WIDE_IN[k]:
            near_b(k, 1)
        if k % 2:
            copies[k]["fAB"] = pass_on(k, -1, AB)

    def to_core(k, r):
        rows_of = pl.ds(0, 2 * half if WIDE_IN[k] else half + piece)
        copies[k]["c", r] = send(xs.at[k, r, rows_of, MINE], xs.at[k, r, rows_of, THEIRS], core)

    def d4a(k):
        wait(k, "upA", "upB", "dnA", "dnB", "upC", "dnC")
        copies[k]["fC"] = pass_on(k, 1 if k % 2 else -1, NEAR if WIDE_IN[k] else NEAR_A)
        to_core(k, 1)
        to_core(k, 3)

    def d5(k):
        wait(k, "fAB", "fC")
        if not WIDE_IN[k]:
            near_b(k, 2)
        to_core(k, 2)

    def d6(k, r):
        if not WIDE_IN[k]:
            wait(k, ("xnB", r))
            copies[k]["cB", r] = send(xs.at[k, r, NEAR_B, MINE], xs.at[k, r, NEAR_B, THEIRS], core)

    def compute(k):
        co = copies[k]
        if k == 0:
            for load in loads:
                load.wait()
        for i, r in enumerate((0, 1, 3, 2)):
            wait(k, *(("c0", "c0C") if r == 0 else (("c", r),)))
            if not WIDE_IN[k]:
                wait(k, ("cB", r))
            pre = jnp.dot(xs[k, r], w_gu[r], preferred_element_type=F32)
            acc[...] = pre if i == 0 else acc[...] + pre
        unit = w_gate.shape[1]
        pre = acc[:, :unit]
        hidden = (pre / (1.0 + jnp.exp(-pre)) * acc[:, unit:]).astype(BF16)
        for r in (2, 1, 3, 0):
            parts[k, r] = jnp.dot(hidden, w_dn[r], preferred_element_type=F32).astype(BF16)
            co["p", r] = send(parts.at[k, r, :, THEIRS], crecv.at[k, r], core)

    def chip_sum(k, r, rows_of):
        return parts[k, r, rows_of, :feat].astype(F32) + crecv[k, r, rows_of].astype(F32)

    def b_sum(k, r):
        if WIDE_OUT[k]:
            return chip_sum(k, r, B)
        return chip_sum(k, r, B) + xb_in[k, r].astype(F32)

    def c_rows(k):
        return NEAR if WIDE_OUT[k] else NEAR_A

    def e(k, r):
        wait(k, ("p", r))
        if not WIDE_OUT[k]:
            xb_out[k, r] = chip_sum(k, r, NEAR_B).astype(BF16)
            copies[k]["xb", r] = send(xb_out.at[k, r], xb_in.at[k, r], x_near)

    def wait_b(k, r):
        wait(k, ("p", r))
        if not WIDE_OUT[k]:
            wait(k, ("xb", r))

    def gC(k):
        wait(k, ("p", 2))
        ring2[k, c_rows(k)] = chip_sum(k, 2, c_rows(k)).astype(BF16)
        copies[k]["gC"] = send(
            ring2.at[k, c_rows(k)], ring2_in.at[k, c_rows(k)], y_up if k % 2 else y_dn
        )

    def gAB(k):
        wait_b(k, 2)
        ring2[k, A] = chip_sum(k, 2, A).astype(BF16)
        ring2[k, B] = b_sum(k, 2).astype(BF16)
        copies[k]["gAB"] = send(ring2.at[k, AB], ring2_in.at[k, AB], y_dn if k % 2 else y_up)

    def way(k, up):
        return (1, ring_up, ring_up_in, y_up) if up else (3, ring_dn, ring_dn_in, y_dn)

    def sC1(k):
        r, buf, into, device = way(k, k % 2 == 0)
        wait(k, ("p", r))
        buf[k, c_rows(k)] = chip_sum(k, r, c_rows(k)).astype(BF16)
        copies[k]["s1C"] = send(buf.at[k, c_rows(k)], into.at[k, c_rows(k)], device)

    def sAB1(k):
        r, buf, into, device = way(k, k % 2 == 1)
        wait_b(k, r)
        buf[k, A] = chip_sum(k, r, A).astype(BF16)
        buf[k, B] = b_sum(k, r).astype(BF16)
        copies[k]["s1AB"] = send(buf.at[k, AB], into.at[k, AB], device)

    def sAB2(k):
        r, buf, into, device = way(k, k % 2 == 0)
        wait_b(k, r)
        wait(k, "gAB")
        buf[k, A] = (chip_sum(k, r, A) + ring2_in[k, A].astype(F32)).astype(BF16)
        buf[k, B] = (b_sum(k, r) + ring2_in[k, B].astype(F32)).astype(BF16)
        copies[k]["s2AB"] = send(buf.at[k, AB], into.at[k, AB], device)

    def sC2(k):
        r, buf, into, device = way(k, k % 2 == 1)
        wait(k, ("p", r), "gC")
        rows_of = c_rows(k)
        buf[k, rows_of] = (chip_sum(k, r, rows_of) + ring2_in[k, rows_of].astype(F32)).astype(BF16)
        copies[k]["s2C"] = send(buf.at[k, rows_of], into.at[k, rows_of], device)

    def neighbours(k, rows_of):
        return ring_up_in[k, rows_of].astype(F32) + ring_dn_in[k, rows_of].astype(F32)

    def rC(k):
        wait(k, ("p", 0), "s1C", "s2C")
        rows_of = c_rows(k)
        into = AB if WIDE_OUT[k] else A
        xn_out[k, into] = (chip_sum(k, 0, rows_of) + neighbours(k, rows_of)).astype(BF16)
        copies[k]["xnback"] = send(xn_out.at[k, into], xn_in.at[k, into], x_near)

    def rAB(k):
        wait_b(k, 0)
        wait(k, "s1AB", "s2AB")
        crossing = b_sum(k, 0) + neighbours(k, B)
        if WIDE_OUT[k]:
            wait(k, "xnback")
            crossing = crossing + xn_in[k, B].astype(F32)
        fin_x[k] = crossing.astype(BF16)
        copies[k]["xcback"] = send(fin_x.at[k], xc_in.at[k], x_cross)
        own[k] = chip_sum(k, 0, A) + neighbours(k, A)

    def r4(k):
        wait(k, "xnback")
        fin[k] = own[k] + xn_in[k, A].astype(F32)

    def r5(k):
        wait(k, "xcback")
        kept = fin[k]
        crossed = xc_in[k].astype(F32)
        for i, j in enumerate(CHUNKS[k]):
            lo, hi = i * cap, (i + 1) * cap
            block = jnp.concatenate([kept[lo:hi], crossed[lo:hi]], axis=0).astype(BF16)
            if j:
                rets[j] = block
                z_back[j] = send(rets.at[j], retr.at[j], at((z + j) % nz, x, y, c))
            else:
                retr[j] = block

    z_back = {}
    STAGES = dict(
        d1=d1, d2=d2, d3=d3, d4u=d4u, d4d=d4d, d4a=d4a, d5=d5, d6=d6, c=compute, e=e, gC=gC, gAB=gAB,
        sC1=sC1, sAB1=sAB1, sAB2=sAB2, sC2=sC2, rC=rC, rAB=rAB, r4=r4, r5=r5,
    )
    for name, *where in ORDER:
        STAGES[name](*where)

    for j in range(1, nz):
        z_back[j].wait_recv()
    back = retr[...].reshape(nz * 2 * cap, feat)
    merged = lax.dot_general(
        slots[...], back, (((0,), (0,)), ((), ())), preferred_element_type=F32
    )
    out[...] = merged.astype(BF16)
    for copy in started:
        copy.wait_send()


def on_device(nx, ny, nz, tokens, routes, router_gate, w_gate, w_up, w_down):
    rows, feat = tokens.shape
    unit = w_gate.shape[1]
    cap = 3 * rows // (nx * nz)
    half, piece = 4 * cap, 2 * cap
    vm = pltpu.VMEM
    scratch = [
        vm((ny, 2 * feat, 2 * unit), BF16),
        vm((ny, unit, 2 * feat), BF16),
        vm((nz * 2 * cap, rows), BF16),
        vm((nz, 2 * cap, feat), BF16),
        vm((nz, 2 * cap, feat), BF16),
        vm((NC, piece, feat), BF16),
        vm((NC, ny, 2 * half, 2 * feat), BF16),
        vm((2 * half, 2 * unit), F32),
        vm((NC, ny, 2 * half, 2 * feat), BF16),
        vm((NC, ny, 2 * half, feat), BF16),
        vm((NC, ny, piece, feat), BF16),
        vm((NC, ny, piece, feat), BF16),
    ]
    scratch += [vm((NC, 2 * half, feat), BF16)] * 6
    scratch += [
        vm((NC, piece, feat), F32),
        vm((NC, half, feat), BF16),
        vm((NC, half, feat), BF16),
        vm((NC, piece, feat), F32),
        vm((NC, piece, feat), BF16),
        vm((NC, piece, feat), BF16),
        vm((nz, 2 * cap, feat), BF16),
        vm((nz, 2 * cap, feat), BF16),
        pltpu.SemaphoreType.DMA((6 * ny,)),
        pltpu.SemaphoreType.DMA((44 * NC + 14,)),
        pltpu.SemaphoreType.DMA((44 * NC + 14,)),
    ]
    in_vmem = pl.BlockSpec(memory_space=pltpu.VMEM)
    in_hbm = pl.BlockSpec(memory_space=pl.ANY)
    return pl.pallas_call(
        functools.partial(kernel, (nx, ny, nz, cap, feat)),
        out_shape=jax.ShapeDtypeStruct((rows, feat), BF16),
        in_specs=[in_vmem] * 3 + [in_hbm] * 3,
        out_specs=in_vmem,
        scratch_shapes=scratch,
        compiler_params=pltpu.CompilerParams(
            collective_id=0, has_side_effects=True, vmem_limit_bytes=60 * 1024 * 1024
        ),
    )(tokens, routes.reshape(1, rows), router_gate.reshape(1, rows), w_gate, w_up, w_down)


def solution(mesh):
    nx, ny = 4, mesh.shape["etp"] // 2
    nz = mesh.shape["ep"] // nx
    return jax.shard_map(
        functools.partial(on_device, nx, ny, nz),
        mesh=mesh,
        in_specs=(
            P("ep", "etp"),
            P("ep", None),
            P("ep", None),
            P(None, ("ep", "etp")),
            P(None, ("ep", "etp")),
            P(("ep", "etp"), None),
        ),
        out_specs=P("ep", "etp"),
        check_vma=False,
    )
```

```python
import functools

import jax
import jax.numpy as jnp
from jax import lax
from jax.experimental import pallas as pl
from jax.experimental.pallas import tpu as pltpu
from jax.sharding import PartitionSpec as P

MESH = pl.DeviceIdType.MESH
F32 = jnp.float32
BF16 = jnp.bfloat16

PAIRS = ((0, 1), (6, 3), (5, 4), (7, 2))
CHUNKS = (
    (0, 0, 16),
    (0, 16, 48),
    (1, 0, 48),
    (2, 0, 48),
    (3, 0, 32),
    (3, 32, 48),
)
WIDE_IN = (0, 0, 0, 0, 0, 0)
WIDE_OUT = (0, 0, 0, 0, 0, 0)
STRAIGHT_IN = (0, 0, 0, 0, 0, 0)
STRAIGHT_OUT = (0, 0, 0, 0, 0, 0)
FLIP = (0, 1, 0, 1, 0, 1)
NC = len(CHUNKS)
SEMS = (49, 102)
Z_ORDER = (1, 7, 6, 2, 3, 5, 4)


ORDER = (
    ("d1", 0), ("d2", 0), ("d3", 0), ("d1", 1), ("d6", 0, 0), ("d4d", 0), ("d4u", 0), ("d4a", 0),
    ("d2", 1), ("d1", 5), ("d1", 4), ("d3", 1), ("d5", 0), ("d2", 5), ("d4u", 1), ("d3", 5),
    ("d2", 4), ("d3", 4), ("d1", 2), ("d4d", 5), ("d6", 0, 1), ("d4a", 1), ("d4a", 5), ("d6", 0, 3),
    ("d6", 5, 0), ("d4d", 1), ("d6", 0, 2), ("d4u", 4), ("d2", 2), ("d1", 3), ("c", 0),
    ("d6", 1, 0), ("d5", 5), ("d4u", 5), ("d5", 1), ("d6", 1, 1), ("d6", 1, 3), ("d6", 4, 0),
    ("d4a", 4), ("d6", 5, 1), ("d4d", 4), ("d3", 2), ("d6", 4, 3), ("d6", 2, 0), ("d2", 3),
    ("d6", 5, 3), ("d6", 5, 2), ("d3", 3), ("d4d", 2), ("d4u", 2), ("d6", 1, 2), ("d5", 4),
    ("c", 5), ("d4a", 2), ("e", 5, 1), ("d4d", 3), ("c", 1), ("d4a", 3), ("d4u", 3), ("d6", 4, 2),
    ("gC", 5), ("d6", 4, 1), ("sC1", 5), ("gC", 0), ("d5", 2), ("e", 1, 2), ("c", 4), ("d5", 3),
    ("e", 5, 2), ("d6", 3, 0), ("sC1", 0), ("gC", 1), ("e", 5, 0), ("d6", 2, 3), ("d6", 2, 1),
    ("d6", 3, 3), ("gC", 4), ("e", 4, 2), ("d6", 2, 2), ("sC1", 4), ("e", 4, 3), ("e", 1, 3),
    ("sC2", 5), ("e", 5, 3), ("gAB", 1), ("c", 2), ("d6", 3, 2), ("gAB", 5), ("sAB1", 5),
    ("e", 2, 2), ("e", 0, 2), ("e", 4, 1), ("e", 2, 1), ("d6", 3, 1), ("sC1", 2), ("gC", 2),
    ("gAB", 4), ("e", 0, 3), ("sAB1", 4), ("c", 3), ("gAB", 2), ("sC2", 4), ("sAB2", 5),
    ("e", 3, 2), ("e", 4, 0), ("e", 2, 3), ("rC", 5), ("gC", 3), ("sC1", 3), ("e", 3, 1),
    ("e", 3, 3), ("sC2", 2), ("gAB", 0), ("e", 2, 0), ("sAB2", 4), ("gAB", 3), ("sAB2", 2),
    ("rAB", 5), ("e", 1, 1), ("sAB1", 2), ("rC", 4), ("sC2", 3), ("r4", 5), ("rAB", 4), ("sAB2", 3),
    ("e", 3, 0), ("sAB1", 3), ("sC2", 0), ("sC1", 1), ("rC", 2), ("sAB1", 1), ("sC2", 1),
    ("rAB", 2), ("r4", 4), ("e", 0, 0), ("r5", 4), ("sAB2", 1), ("r5", 5), ("e", 0, 1), ("e", 1, 0),
    ("rC", 3), ("rC", 0), ("rAB", 3), ("r4", 2), ("r5", 2), ("sAB2", 0), ("sAB1", 0), ("r4", 3),
    ("rAB", 1), ("rC", 1), ("r5", 3), ("rAB", 0), ("r4", 1), ("r4", 0), ("r5", 0), ("r5", 1),
)

BACK = {"up": "dn", "dn": "up", "two": "two", "core": "core", "near": "near", "cross": "cross"}


def kernel(sizes, tokens, routes, gate, w_gate, w_up, w_down, out,
           w_gu, w_dn, outgo, zrecv, cross, xs, acc, parts, crecv, xb_out, xb_in,
           ring2, ring2_in, ring_up, ring_up_in, ring_dn, ring_dn_in,
           own, xn_out, xn_in, fin, fin_x, xc_in, rets, retr, tok, slots_t,
           t_sem, w_sem, send_sem, recv_sem):
    nx, ny, nz, cap, feat = sizes
    ep = lax.axis_index("ep")
    etp = lax.axis_index("etp")
    z, x = ep // nx, ep % nx
    y, c = etp // 2, etp % 2

    def at(zz, xx, yy, cc):
        return {"ep": zz * nx + xx, "etp": yy * 2 + cc}

    y_up, y_dn = ("up", at(z, x, (y + 1) % ny, c)), ("dn", at(z, x, (y + ny - 1) % ny, c))
    y_two = ("two", at(z, x, (y + 2) % ny, c))
    core = ("core", at(z, x, y, 1 - c))
    x_near = ("near", at(z, x + 1 - 2 * (x % 2), y, c))
    x_cross = ("cross", at(z, nx - 1 - x, y, c))

    load_tokens = pltpu.make_async_copy(tokens, tok, t_sem)
    load_tokens.start()
    barrier = pltpu.get_barrier_semaphore()
    peers = [to[1] for to in (y_up, y_dn, core, x_near, x_cross)]
    if any(STRAIGHT_IN + STRAIGHT_OUT):
        peers.append(y_two[1])
    peers += [at((z + j) % nz, x, y, c) for j in range(1, nz)]
    for peer in peers:
        pl.semaphore_signal(barrier, inc=1, device_id=peer, device_id_type=MESH)

    rows = routes.shape[1]
    expert = routes[...]
    onehot = (expert == lax.broadcasted_iota(jnp.int32, (nz * nx // 2, rows), 0)).astype(F32)
    before = lax.broadcasted_iota(jnp.int32, (rows, rows), 0) < lax.broadcasted_iota(
        jnp.int32, (rows, rows), 1
    )
    ranks = jnp.dot(onehot.astype(BF16), before.astype(F32).astype(BF16), preferred_element_type=F32)
    rank = jnp.sum(ranks * onehot, axis=0, keepdims=True).astype(jnp.int32)
    unit_of = (z + nz - (expert >> 1)) & (nz - 1)
    other = (expert & 1) != x // 2
    slot = unit_of * (2 * cap) + jnp.where(other, cap, 0) + rank
    place = lax.broadcasted_iota(jnp.int32, (nz * 2 * cap, rows), 0)
    chosen = (slot == place).astype(F32)
    load_tokens.wait()
    sent = jnp.dot(chosen.astype(BF16), tok[...], preferred_element_type=F32)
    outgo[...] = sent.astype(BF16).reshape(nz, 2 * cap, feat)
    clock, used = [0], [0, 0]
    heard = dict.fromkeys(BACK, -1)
    free_send, free_recv = [], []

    def send(src, dst, to):
        link, device = to
        clock[0] += 1
        if free_send:
            i = free_send.pop()
        else:
            i = used[0]
            used[0] += 1
        ready = [at_ for at_ in free_recv if link in BACK and at_[0] < heard[BACK[link]]]
        if ready:
            free_recv.remove(ready[0])
            j = ready[0][1]
        else:
            j = used[1]
            used[1] += 1
        copy = pltpu.make_async_remote_copy(
            src_ref=src, dst_ref=dst, send_sem=send_sem.at[i], recv_sem=recv_sem.at[j],
            device_id=device, device_id_type=MESH,
        )
        copy.start()
        return copy, link, clock[0], i, j

    def finish(flight):
        copy, link, sent_at, i, j = flight
        copy.wait_recv()
        copy.wait_send()
        clock[0] += 1
        if link in BACK:
            heard[link] = max(heard[link], sent_at)
        free_send.append(i)
        free_recv.append((clock[0], j))

    pl.semaphore_wait(barrier, len(peers))

    z_copy = {}
    for j in Z_ORDER:
        z_copy[j] = send(outgo.at[j], zrecv.at[j], ("z", at((z + nz - j) % nz, x, y, c)))

    unit = w_gate.shape[1]
    for r in range(ny):
        for k in range(2):
            shard = pl.ds(pl.multiple_of((((y + r) % ny) * 2 + (c + k) % 2) * feat, 128), feat)
            into = pl.ds(k * feat, feat)
            for source, target, sem in (
                (w_gate.at[shard, :], w_gu.at[r, into, pl.ds(0, unit)], 0),
                (w_up.at[shard, :], w_gu.at[r, into, pl.ds(unit, unit)], 0),
                (w_down.at[:, shard], w_dn.at[r, :, into], 1),
            ):
                pltpu.make_async_copy(source, target, w_sem.at[sem]).start()
    loads = [pltpu.make_async_copy(w, w, w_sem.at[i]) for i, w in enumerate((w_gu, w_dn))]

    slots_t[...] = (chosen * gate[...].astype(F32)).T.astype(BF16)

    MINE, THEIRS = pl.ds(0, feat), pl.ds(feat, feat)
    n_of = [hi - lo for _, lo, hi in CHUNKS]

    def A(k):
        return pl.ds(0, n_of[k])

    def B(k):
        return pl.ds(n_of[k], n_of[k])

    def AB(k):
        return pl.ds(0, 2 * n_of[k])

    def NEAR_A(k):
        return pl.ds(2 * n_of[k], n_of[k])

    def NEAR_B(k):
        return pl.ds(3 * n_of[k], n_of[k])

    def C_IN(k):
        return pl.ds(2 * n_of[k], (2 if WIDE_IN[k] else 1) * n_of[k])

    def C_OUT(k):
        return pl.ds(2 * n_of[k], (2 if WIDE_OUT[k] else 1) * n_of[k])

    copies = [dict() for _ in CHUNKS]

    def wait(k, *names):
        for name in names:
            flight = copies[k][name]
            if flight is not None:
                finish(flight)
                copies[k][name] = None

    def take(k, off):
        pair, lo, hi = CHUNKS[k]
        found = []
        for i, j in enumerate(PAIRS[pair]):
            first, last = max(lo - i * cap, 0), min(hi - i * cap, cap)
            if first < last:
                if j in z_copy:
                    finish(z_copy.pop(j))
                block = (zrecv if j else outgo)[j].astype(F32)
                found.append(block[off + first : off + last])
        return jnp.concatenate(found, axis=0).astype(BF16) if len(found) > 1 else found[0].astype(BF16)

    def d1(k):
        co = copies[k]
        cross[k, A(k)] = take(k, cap)
        co["cross"] = send(cross.at[k, A(k)], xs.at[k, 0, B(k), MINE], x_cross)
        xs[k, 0, A(k), :feat] = take(k, 0)
        mine = xs.at[k, 0, A(k), MINE]
        co["xnA"] = send(mine, xs.at[k, 0, NEAR_A(k), MINE], x_near)
        co["upA"] = send(mine, xs.at[k, 3, A(k), MINE], y_up)
        co["dnA"] = send(mine, xs.at[k, 1, A(k), MINE], y_dn)
        if STRAIGHT_IN[k]:
            co["y2A"] = send(mine, xs.at[k, 2, A(k), MINE], y_two)

    def near_b(k, r):
        copies[k]["xnB", r] = send(xs.at[k, r, B(k), MINE], xs.at[k, r, NEAR_B(k), MINE], x_near)

    def d2(k):
        co = copies[k]
        wait(k, "cross")
        near_b(k, 0)
        mine = xs.at[k, 0, B(k), MINE]
        co["upB"] = send(mine, xs.at[k, 3, B(k), MINE], y_up)
        co["dnB"] = send(mine, xs.at[k, 1, B(k), MINE], y_dn)
        if STRAIGHT_IN[k]:
            co["y2B"] = send(mine, xs.at[k, 2, B(k), MINE], y_two)
        co["c0"] = send(xs.at[k, 0, AB(k), MINE], xs.at[k, 0, AB(k), THEIRS], core)

    def d3(k):
        co = copies[k]
        wait(k, "xnA")
        if WIDE_IN[k]:
            wait(k, ("xnB", 0))
        rows_c = C_IN(k)
        mine = xs.at[k, 0, rows_c, MINE]
        co["upC"] = send(mine, xs.at[k, 3, rows_c, MINE], y_up)
        co["dnC"] = send(mine, xs.at[k, 1, rows_c, MINE], y_dn)
        if STRAIGHT_IN[k]:
            co["y2C"] = send(mine, xs.at[k, 2, rows_c, MINE], y_two)
        co["c0C"] = send(mine, xs.at[k, 0, rows_c, THEIRS], core)

    def pass_on(k, up, rows_of):
        src, device = (3, y_up) if up else (1, y_dn)
        return send(xs.at[k, src, rows_of, MINE], xs.at[k, 2, rows_of, MINE], device)

    def up_AB(k):
        return not FLIP[k]

    def d4u(k):
        wait(k, "upA", "upB")
        if not WIDE_IN[k]:
            near_b(k, 3)
        if up_AB(k) and not STRAIGHT_IN[k]:
            copies[k]["fAB"] = pass_on(k, True, AB(k))

    def d4d(k):
        wait(k, "dnA", "dnB")
        if not WIDE_IN[k]:
            near_b(k, 1)
        if not up_AB(k) and not STRAIGHT_IN[k]:
            copies[k]["fAB"] = pass_on(k, False, AB(k))

    def to_core(k, r):
        rows_of = pl.ds(0, (4 if WIDE_IN[k] else 3) * n_of[k])
        copies[k]["c", r] = send(xs.at[k, r, rows_of, MINE], xs.at[k, r, rows_of, THEIRS], core)

    def d4a(k):
        wait(k, "upA", "upB", "dnA", "dnB", "upC", "dnC")
        if not STRAIGHT_IN[k]:
            copies[k]["fC"] = pass_on(k, not up_AB(k), C_IN(k))
        to_core(k, 1)
        to_core(k, 3)

    def d5(k):
        wait(k, *(("y2A", "y2B", "y2C") if STRAIGHT_IN[k] else ("fAB", "fC")))
        if not WIDE_IN[k]:
            near_b(k, 2)
        to_core(k, 2)

    def d6(k, r):
        if not WIDE_IN[k]:
            wait(k, ("xnB", r))
            mine = xs.at[k, r, NEAR_B(k), MINE]
            copies[k]["cB", r] = send(mine, xs.at[k, r, NEAR_B(k), THEIRS], core)

    def compute(k):
        co = copies[k]
        while loads:
            loads.pop().wait()
        whole = pl.ds(0, 4 * n_of[k])
        for i, r in enumerate((0, 1, 3, 2)):
            wait(k, *(("c0", "c0C") if r == 0 else (("c", r),)))
            if not WIDE_IN[k]:
                wait(k, ("cB", r))
            pre = jnp.dot(xs[k, r, whole, :], w_gu[r], preferred_element_type=F32)
            acc[whole, :] = pre if i == 0 else acc[whole, :] + pre
        unit = w_gate.shape[1]
        pre = acc[whole, :unit]
        hidden = (pre / (1.0 + jnp.exp(-pre)) * acc[whole, unit:]).astype(BF16)
        for r in (2, 1, 3, 0):
            parts[k, r, whole, :] = jnp.dot(
                hidden, w_dn[r], preferred_element_type=F32
            ).astype(BF16)
            co["p", r] = send(parts.at[k, r, whole, THEIRS], crecv.at[k, r, whole], core)

    def chip_sum(k, r, rows_of):
        return parts[k, r, rows_of, :feat].astype(F32) + crecv[k, r, rows_of].astype(F32)

    def b_sum(k, r):
        if WIDE_OUT[k]:
            return chip_sum(k, r, B(k))
        return chip_sum(k, r, B(k)) + xb_in[k, r, A(k)].astype(F32)

    def e(k, r):
        wait(k, ("p", r))
        if not WIDE_OUT[k]:
            xb_out[k, r, A(k)] = chip_sum(k, r, NEAR_B(k)).astype(BF16)
            copies[k]["xb", r] = send(xb_out.at[k, r, A(k)], xb_in.at[k, r, A(k)], x_near)

    def wait_b(k, r):
        wait(k, ("p", r))
        if not WIDE_OUT[k]:
            wait(k, ("xb", r))

    def gC(k):
        wait(k, ("p", 2))
        rows_of = C_OUT(k)
        ring2[k, rows_of] = chip_sum(k, 2, rows_of).astype(BF16)
        device = y_two if STRAIGHT_OUT[k] else y_dn if up_AB(k) else y_up
        copies[k]["gC"] = send(ring2.at[k, rows_of], ring2_in.at[k, rows_of], device)

    def gAB(k):
        wait_b(k, 2)
        ring2[k, A(k)] = chip_sum(k, 2, A(k)).astype(BF16)
        ring2[k, B(k)] = b_sum(k, 2).astype(BF16)
        device = y_two if STRAIGHT_OUT[k] else y_up if up_AB(k) else y_dn
        copies[k]["gAB"] = send(ring2.at[k, AB(k)], ring2_in.at[k, AB(k)], device)

    def way(k, up):
        return (1, ring_up, ring_up_in, y_up) if up else (3, ring_dn, ring_dn_in, y_dn)

    def passing(k, name, rows_of):
        if STRAIGHT_OUT[k]:
            return 0.0
        wait(k, name)
        return ring2_in[k, rows_of].astype(F32)

    def sC1(k):
        r, buf, into, device = way(k, up_AB(k))
        wait(k, ("p", r))
        rows_of = C_OUT(k)
        buf[k, rows_of] = chip_sum(k, r, rows_of).astype(BF16)
        copies[k]["s1C"] = send(buf.at[k, rows_of], into.at[k, rows_of], device)

    def sAB1(k):
        r, buf, into, device = way(k, not up_AB(k))
        wait_b(k, r)
        buf[k, A(k)] = chip_sum(k, r, A(k)).astype(BF16)
        buf[k, B(k)] = b_sum(k, r).astype(BF16)
        copies[k]["s1AB"] = send(buf.at[k, AB(k)], into.at[k, AB(k)], device)

    def sAB2(k):
        r, buf, into, device = way(k, up_AB(k))
        wait_b(k, r)
        buf[k, A(k)] = (chip_sum(k, r, A(k)) + passing(k, "gAB", A(k))).astype(BF16)
        buf[k, B(k)] = (b_sum(k, r) + passing(k, "gAB", B(k))).astype(BF16)
        copies[k]["s2AB"] = send(buf.at[k, AB(k)], into.at[k, AB(k)], device)

    def sC2(k):
        r, buf, into, device = way(k, not up_AB(k))
        wait(k, ("p", r))
        rows_of = C_OUT(k)
        buf[k, rows_of] = (chip_sum(k, r, rows_of) + passing(k, "gC", rows_of)).astype(BF16)
        copies[k]["s2C"] = send(buf.at[k, rows_of], into.at[k, rows_of], device)

    def neighbours(k, rows_of):
        both = ring_up_in[k, rows_of].astype(F32) + ring_dn_in[k, rows_of].astype(F32)
        if STRAIGHT_OUT[k]:
            both = both + ring2_in[k, rows_of].astype(F32)
        return both

    def rC(k):
        wait(k, ("p", 0), "s1C", "s2C")
        if STRAIGHT_OUT[k]:
            wait(k, "gC")
        rows_of = C_OUT(k)
        into = AB(k) if WIDE_OUT[k] else A(k)
        xn_out[k, into] = (chip_sum(k, 0, rows_of) + neighbours(k, rows_of)).astype(BF16)
        copies[k]["xnback"] = send(xn_out.at[k, into], xn_in.at[k, into], x_near)

    def rAB(k):
        pair, lo, hi = CHUNKS[k]
        wait_b(k, 0)
        wait(k, "s1AB", "s2AB")
        if STRAIGHT_OUT[k]:
            wait(k, "gAB")
        crossing = b_sum(k, 0) + neighbours(k, B(k))
        if WIDE_OUT[k]:
            wait(k, "xnback")
            crossing = crossing + xn_in[k, B(k)].astype(F32)
        fin_x[k, A(k)] = crossing.astype(BF16)
        copies[k]["xcback"] = send(
            fin_x.at[k, A(k)], xc_in.at[pair, pl.ds(lo, hi - lo)], x_cross
        )
        own[k, A(k)] = chip_sum(k, 0, A(k)) + neighbours(k, A(k))

    def r4(k):
        pair, lo, hi = CHUNKS[k]
        wait(k, "xnback")
        fin[pair, lo:hi] = own[k, A(k)] + xn_in[k, A(k)].astype(F32)

    def r5(k):
        wait(k, "xcback")
        pair, lo, hi = CHUNKS[k]
        for i, j in enumerate(PAIRS[pair]):
            first, last = i * cap, (i + 1) * cap
            if lo < last <= hi:
                kept, crossed = fin[pair, first:last], xc_in[pair, first:last].astype(F32)
                block = jnp.concatenate([kept, crossed], axis=0).astype(BF16)
                if j:
                    rets[j] = block
                    z_back[j] = send(rets.at[j], retr.at[j], ("z", at((z + j) % nz, x, y, c)))
                else:
                    retr[j] = block

    z_back = {}
    STAGES = dict(
        d1=d1, d2=d2, d3=d3, d4u=d4u, d4d=d4d, d4a=d4a, d5=d5, d6=d6, c=compute, e=e, gC=gC, gAB=gAB,
        sC1=sC1, sAB1=sAB1, sAB2=sAB2, sC2=sC2, rC=rC, rAB=rAB, r4=r4, r5=r5,
    )
    for name, *where in ORDER:
        STAGES[name](*where)

    for j in range(1, nz):
        finish(z_back[j])
    back = retr[...].reshape(nz * 2 * cap, feat)
    merged = jnp.dot(slots_t[...], back, preferred_element_type=F32)
    out[...] = merged.astype(BF16)


def on_device(nx, ny, nz, tokens, routes, router_gate, w_gate, w_up, w_down):
    rows, feat = tokens.shape
    unit = w_gate.shape[1]
    cap = 3 * rows // (nx * nz)
    half, piece = 4 * cap, 2 * cap
    vm = pltpu.VMEM
    scratch = [
        vm((ny, 2 * feat, 2 * unit), BF16),
        vm((ny, unit, 2 * feat), BF16),
        vm((nz, 2 * cap, feat), BF16),
        vm((nz, 2 * cap, feat), BF16),
        vm((NC, piece, feat), BF16),
        vm((NC, ny, 2 * half, 2 * feat), BF16),
        vm((2 * half, 2 * unit), F32),
        vm((NC, ny, 2 * half, 2 * feat), BF16),
        vm((NC, ny, 2 * half, feat), BF16),
        vm((NC, ny, piece, feat), BF16),
        vm((NC, ny, piece, feat), BF16),
    ]
    scratch += [vm((NC, 2 * half, feat), BF16)] * 6
    scratch += [
        vm((NC, piece, feat), F32),
        vm((NC, half, feat), BF16),
        vm((NC, half, feat), BF16),
        vm((len(PAIRS), piece, feat), F32),
        vm((NC, piece, feat), BF16),
        vm((len(PAIRS), piece, feat), BF16),
        vm((nz, 2 * cap, feat), BF16),
        vm((nz, 2 * cap, feat), BF16),
        vm((rows, feat), BF16),
        vm((rows, nz * 2 * cap), BF16),
        pltpu.SemaphoreType.DMA,
        pltpu.SemaphoreType.DMA((2,)),
        pltpu.SemaphoreType.DMA((SEMS[0],)),
        pltpu.SemaphoreType.DMA((SEMS[1],)),
    ]
    in_vmem = pl.BlockSpec(memory_space=pltpu.VMEM)
    in_hbm = pl.BlockSpec(memory_space=pl.ANY)
    return pl.pallas_call(
        functools.partial(kernel, (nx, ny, nz, cap, feat)),
        out_shape=jax.ShapeDtypeStruct((rows, feat), BF16),
        in_specs=[in_hbm] + [in_vmem] * 2 + [in_hbm] * 3,
        out_specs=in_vmem,
        scratch_shapes=scratch,
        compiler_params=pltpu.CompilerParams(
            collective_id=0, has_side_effects=True, vmem_limit_bytes=60 * 1024 * 1024
        ),
    )(tokens, routes.reshape(1, rows), router_gate.reshape(1, rows), w_gate, w_up, w_down)


def solution(mesh):
    nx, ny = 4, mesh.shape["etp"] // 2
    nz = mesh.shape["ep"] // nx
    return jax.shard_map(
        functools.partial(on_device, nx, ny, nz),
        mesh=mesh,
        in_specs=(
            P("ep", "etp"),
            P("ep", None),
            P("ep", None),
            P(None, ("ep", "etp")),
            P(None, ("ep", "etp")),
            P(("ep", "etp"), None),
        ),
        out_specs=P("ep", "etp"),
        check_vma=False,
    )
```

```python
import functools

import jax
import jax.numpy as jnp
from jax import lax
from jax.experimental import pallas as pl
from jax.experimental.pallas import tpu as pltpu
from jax.sharding import PartitionSpec as P

MESH = pl.DeviceIdType.MESH
F32 = jnp.float32
BF16 = jnp.bfloat16

PAIRS = ((0, 1), (6, 3), (5, 4), (7, 2))
CHUNKS = (
    (0, 0, 16),
    (0, 16, 48),
    (1, 0, 48),
    (2, 0, 48),
    (3, 0, 32),
    (3, 32, 48),
)
WIDE_IN = (0, 0, 0, 0, 0, 0)
WIDE_OUT = (0, 0, 0, 0, 1, 0)
STRAIGHT_IN = (0, 0, 0, 0, 0, 0)
STRAIGHT_OUT = (0, 0, 0, 0, 0, 0)
FLIP = (0, 1, 0, 1, 0, 1)
NC = len(CHUNKS)
SEMS = (49, 103)
Z_ORDER = (1, 7, 6, 2, 3, 5, 4)


ORDER = (
    ("d1", 0), ("d2", 0), ("d3", 0), ("d1", 1), ("d4u", 0), ("d4d", 0), ("d4a", 0), ("d2", 1),
    ("d1", 5), ("d1", 4), ("d3", 1), ("d5", 0), ("d2", 5), ("d6", 0, 3), ("d6", 0, 0), ("d6", 0, 1),
    ("d6", 1, 0), ("d4u", 1), ("d3", 5), ("d2", 4), ("d3", 4), ("d1", 2), ("d6", 5, 0), ("d4u", 5),
    ("d4a", 5), ("d4d", 5), ("d4u", 4), ("d6", 0, 2), ("d4d", 4), ("d4a", 4), ("d2", 2),
    ("d6", 5, 1), ("d3", 2), ("d1", 3), ("c", 0), ("d5", 4), ("d6", 4, 3), ("d5", 5), ("d6", 4, 0),
    ("d4u", 2), ("d2", 3), ("d4d", 2), ("d6", 4, 1), ("d6", 4, 2), ("d4a", 2), ("d3", 3),
    ("d4a", 1), ("d4d", 1), ("c", 4), ("sC1", 0), ("d4d", 3), ("d6", 2, 3), ("gC", 4), ("d6", 5, 2),
    ("d5", 2), ("sAB1", 4), ("e", 0, 2), ("d6", 5, 3), ("d4u", 3), ("e", 0, 1), ("d6", 2, 0),
    ("d6", 1, 1), ("d4a", 3), ("sC1", 4), ("c", 5), ("gAB", 4), ("d6", 2, 2), ("d6", 2, 1),
    ("gC", 5), ("e", 5, 2), ("d6", 3, 1), ("e", 5, 1), ("gAB", 0), ("gC", 0), ("d5", 3), ("d5", 1),
    ("c", 2), ("sC1", 5), ("d6", 3, 3), ("e", 5, 3), ("gC", 2), ("e", 2, 2), ("sC2", 4), ("sC1", 2),
    ("gAB", 5), ("d6", 3, 2), ("d6", 3, 0), ("e", 2, 3), ("e", 5, 0), ("sC2", 5), ("e", 2, 1),
    ("d6", 1, 3), ("sAB2", 4), ("c", 3), ("sC2", 2), ("gAB", 2), ("sAB1", 5), ("e", 3, 2),
    ("rC", 5), ("sAB1", 2), ("d6", 1, 2), ("rC", 4), ("gC", 3), ("e", 3, 3), ("e", 3, 1),
    ("sAB2", 5), ("c", 1), ("gAB", 3), ("e", 2, 0), ("sAB2", 2), ("sC1", 3), ("rAB", 4),
    ("e", 1, 2), ("r4", 4), ("rC", 2), ("e", 0, 3), ("rAB", 5), ("sC2", 0), ("gC", 1), ("r4", 5),
    ("sC2", 3), ("sAB1", 3), ("e", 3, 0), ("sAB2", 3), ("rAB", 2), ("e", 1, 1), ("e", 1, 3),
    ("gAB", 1), ("sAB2", 0), ("rC", 3), ("sC1", 1), ("e", 1, 0), ("r4", 2), ("sC2", 1), ("sAB1", 0),
    ("rC", 0), ("e", 0, 0), ("rAB", 3), ("sAB1", 1), ("sAB2", 1), ("r4", 3), ("rC", 1), ("rAB", 0),
    ("rAB", 1), ("r4", 0), ("r4", 1),
)

BACK = {"up": "dn", "dn": "up", "two": "two", "core": "core", "near": "near", "cross": "cross"}


def kernel(sizes, tokens, routes, gate, w_gate, w_up, w_down, out,
           w_gu, w_dn, outgo, zrecv, cross, xs, acc, parts, crecv, xb_out, xb_in,
           ring2, ring2_in, ring_up, ring_up_in, ring_dn, ring_dn_in,
           own, xn_out, xn_in, fin, fin_x, ret_own, ret_x, retr, tok, slots_t,
           t_sem, w_sem, send_sem, recv_sem):
    nx, ny, nz, cap, feat = sizes
    tall = -(-cap // 16) * 16
    ep = lax.axis_index("ep")
    etp = lax.axis_index("etp")
    z, x = ep // nx, ep % nx
    y, c = etp // 2, etp % 2

    def at(zz, xx, yy, cc):
        return {"ep": zz * nx + xx, "etp": yy * 2 + cc}

    y_up, y_dn = ("up", at(z, x, (y + 1) % ny, c)), ("dn", at(z, x, (y + ny - 1) % ny, c))
    y_two = ("two", at(z, x, (y + 2) % ny, c))
    core = ("core", at(z, x, y, 1 - c))
    x_near = ("near", at(z, x + 1 - 2 * (x % 2), y, c))
    x_cross = ("cross", at(z, nx - 1 - x, y, c))

    load_tokens = pltpu.make_async_copy(tokens, tok, t_sem)
    load_tokens.start()
    barrier = pltpu.get_barrier_semaphore()
    peers = [to[1] for to in (y_up, y_dn, core, x_near, x_cross)]
    if any(STRAIGHT_IN + STRAIGHT_OUT):
        peers.append(y_two[1])
    peers += [at((z + j) % nz, xx, y, c) for j in range(1, nz) for xx in (x, nx - 1 - x)]
    for peer in peers:
        pl.semaphore_signal(barrier, inc=1, device_id=peer, device_id_type=MESH)

    rows = routes.shape[1]
    expert = routes[...]
    onehot = (expert == lax.broadcasted_iota(jnp.int32, (nz * nx // 2, rows), 0)).astype(F32)
    before = lax.broadcasted_iota(jnp.int32, (rows, rows), 0) < lax.broadcasted_iota(
        jnp.int32, (rows, rows), 1
    )
    ranks = jnp.dot(onehot.astype(BF16), before.astype(F32).astype(BF16), preferred_element_type=F32)
    rank = jnp.sum(ranks * onehot, axis=0, keepdims=True).astype(jnp.int32)
    unit_of = (z + nz - (expert >> 1)) & (nz - 1)
    other = (expert & 1) != x // 2
    slot = unit_of * (2 * cap) + jnp.where(other, cap, 0) + rank
    place = lax.broadcasted_iota(jnp.int32, (nz * 2 * cap, rows), 0)
    chosen = (slot == place).astype(F32)
    load_tokens.wait()
    sent = jnp.dot(chosen.astype(BF16), tok[...], preferred_element_type=F32)
    outgo[...] = sent.astype(BF16).reshape(nz, 2 * cap, feat)
    clock, used = [0], [0, 0]
    heard = dict.fromkeys(BACK, -1)
    free_send, free_recv = [], []

    def send(src, dst, to):
        link, device = to
        clock[0] += 1
        if free_send:
            i = free_send.pop()
        else:
            i = used[0]
            used[0] += 1
        ready = [at_ for at_ in free_recv if link in BACK and at_[0] < heard[BACK[link]]]
        if ready:
            free_recv.remove(ready[0])
            j = ready[0][1]
        else:
            j = used[1]
            used[1] += 1
        copy = pltpu.make_async_remote_copy(
            src_ref=src, dst_ref=dst, send_sem=send_sem.at[i], recv_sem=recv_sem.at[j],
            device_id=device, device_id_type=MESH,
        )
        copy.start()
        return copy, link, clock[0], i, j

    def finish(flight):
        copy, link, sent_at, i, j = flight
        copy.wait_recv()
        copy.wait_send()
        clock[0] += 1
        if link in BACK:
            heard[link] = max(heard[link], sent_at)
        free_send.append(i)
        free_recv.append((clock[0], j))

    pl.semaphore_wait(barrier, len(peers))

    z_copy = {}
    for j in Z_ORDER:
        z_copy[j] = send(outgo.at[j], zrecv.at[j], ("z", at((z + nz - j) % nz, x, y, c)))

    unit = w_gate.shape[1]
    for r in range(ny):
        for k in range(2):
            shard = pl.ds(pl.multiple_of((((y + r) % ny) * 2 + (c + k) % 2) * feat, 128), feat)
            into = pl.ds(k * feat, feat)
            for source, target, sem in (
                (w_gate.at[shard, :], w_gu.at[r, into, pl.ds(0, unit)], 0),
                (w_up.at[shard, :], w_gu.at[r, into, pl.ds(unit, unit)], 0),
                (w_down.at[:, shard], w_dn.at[r, :, into], 1),
            ):
                pltpu.make_async_copy(source, target, w_sem.at[sem]).start()
    loads = [pltpu.make_async_copy(w, w, w_sem.at[i]) for i, w in enumerate((w_gu, w_dn))]

    back_slot = unit_of * (2 * tall) + jnp.where(other, tall, 0) + rank
    back_place = lax.broadcasted_iota(jnp.int32, (nz * 2 * tall, rows), 0)
    weighted = jnp.where(back_slot == back_place, gate[...].astype(F32), 0.0)
    slots_t[...] = weighted.T.astype(BF16)

    MINE, THEIRS = pl.ds(0, feat), pl.ds(feat, feat)
    n_of = [hi - lo for _, lo, hi in CHUNKS]

    def A(k):
        return pl.ds(0, n_of[k])

    def B(k):
        return pl.ds(n_of[k], n_of[k])

    def AB(k):
        return pl.ds(0, 2 * n_of[k])

    def NEAR_A(k):
        return pl.ds(2 * n_of[k], n_of[k])

    def NEAR_B(k):
        return pl.ds(3 * n_of[k], n_of[k])

    def C_IN(k):
        return pl.ds(2 * n_of[k], (2 if WIDE_IN[k] else 1) * n_of[k])

    def C_OUT(k):
        return pl.ds(2 * n_of[k], (2 if WIDE_OUT[k] else 1) * n_of[k])

    copies = [dict() for _ in CHUNKS]

    def wait(k, *names):
        for name in names:
            flight = copies[k][name]
            if flight is not None:
                finish(flight)
                copies[k][name] = None

    def take(k, off):
        pair, lo, hi = CHUNKS[k]
        found = []
        for i, j in enumerate(PAIRS[pair]):
            first, last = max(lo - i * cap, 0), min(hi - i * cap, cap)
            if first < last:
                if j in z_copy:
                    finish(z_copy.pop(j))
                block = (zrecv if j else outgo)[j].astype(F32)
                found.append(block[off + first : off + last])
        return jnp.concatenate(found, axis=0).astype(BF16) if len(found) > 1 else found[0].astype(BF16)

    def d1(k):
        co = copies[k]
        cross[k, A(k)] = take(k, cap)
        co["cross"] = send(cross.at[k, A(k)], xs.at[k, 0, B(k), MINE], x_cross)
        xs[k, 0, A(k), :feat] = take(k, 0)
        mine = xs.at[k, 0, A(k), MINE]
        co["xnA"] = send(mine, xs.at[k, 0, NEAR_A(k), MINE], x_near)
        co["upA"] = send(mine, xs.at[k, 3, A(k), MINE], y_up)
        co["dnA"] = send(mine, xs.at[k, 1, A(k), MINE], y_dn)
        if STRAIGHT_IN[k]:
            co["y2A"] = send(mine, xs.at[k, 2, A(k), MINE], y_two)

    def near_b(k, r):
        copies[k]["xnB", r] = send(xs.at[k, r, B(k), MINE], xs.at[k, r, NEAR_B(k), MINE], x_near)

    def d2(k):
        co = copies[k]
        wait(k, "cross")
        near_b(k, 0)
        mine = xs.at[k, 0, B(k), MINE]
        co["upB"] = send(mine, xs.at[k, 3, B(k), MINE], y_up)
        co["dnB"] = send(mine, xs.at[k, 1, B(k), MINE], y_dn)
        if STRAIGHT_IN[k]:
            co["y2B"] = send(mine, xs.at[k, 2, B(k), MINE], y_two)
        co["c0"] = send(xs.at[k, 0, AB(k), MINE], xs.at[k, 0, AB(k), THEIRS], core)

    def d3(k):
        co = copies[k]
        wait(k, "xnA")
        if WIDE_IN[k]:
            wait(k, ("xnB", 0))
        rows_c = C_IN(k)
        mine = xs.at[k, 0, rows_c, MINE]
        co["upC"] = send(mine, xs.at[k, 3, rows_c, MINE], y_up)
        co["dnC"] = send(mine, xs.at[k, 1, rows_c, MINE], y_dn)
        if STRAIGHT_IN[k]:
            co["y2C"] = send(mine, xs.at[k, 2, rows_c, MINE], y_two)
        co["c0C"] = send(mine, xs.at[k, 0, rows_c, THEIRS], core)

    def pass_on(k, up, rows_of):
        src, device = (3, y_up) if up else (1, y_dn)
        return send(xs.at[k, src, rows_of, MINE], xs.at[k, 2, rows_of, MINE], device)

    def up_AB(k):
        return not FLIP[k]

    def d4u(k):
        wait(k, "upA", "upB")
        if not WIDE_IN[k]:
            near_b(k, 3)
        if up_AB(k) and not STRAIGHT_IN[k]:
            copies[k]["fAB"] = pass_on(k, True, AB(k))

    def d4d(k):
        wait(k, "dnA", "dnB")
        if not WIDE_IN[k]:
            near_b(k, 1)
        if not up_AB(k) and not STRAIGHT_IN[k]:
            copies[k]["fAB"] = pass_on(k, False, AB(k))

    def to_core(k, r):
        rows_of = pl.ds(0, (4 if WIDE_IN[k] else 3) * n_of[k])
        copies[k]["c", r] = send(xs.at[k, r, rows_of, MINE], xs.at[k, r, rows_of, THEIRS], core)

    def d4a(k):
        wait(k, "upA", "upB", "dnA", "dnB", "upC", "dnC")
        if not STRAIGHT_IN[k]:
            copies[k]["fC"] = pass_on(k, not up_AB(k), C_IN(k))
        to_core(k, 1)
        to_core(k, 3)

    def d5(k):
        wait(k, *(("y2A", "y2B", "y2C") if STRAIGHT_IN[k] else ("fAB", "fC")))
        if not WIDE_IN[k]:
            near_b(k, 2)
        to_core(k, 2)

    def d6(k, r):
        if not WIDE_IN[k]:
            wait(k, ("xnB", r))
            mine = xs.at[k, r, NEAR_B(k), MINE]
            copies[k]["cB", r] = send(mine, xs.at[k, r, NEAR_B(k), THEIRS], core)

    def compute(k):
        co = copies[k]
        while loads:
            loads.pop().wait()
        whole = pl.ds(0, 4 * n_of[k])
        for i, r in enumerate((0, 1, 3, 2)):
            wait(k, *(("c0", "c0C") if r == 0 else (("c", r),)))
            if not WIDE_IN[k]:
                wait(k, ("cB", r))
            pre = jnp.dot(xs[k, r, whole, :], w_gu[r], preferred_element_type=F32)
            acc[whole, :] = pre if i == 0 else acc[whole, :] + pre
        unit = w_gate.shape[1]
        pre = acc[whole, :unit]
        hidden = (pre / (1.0 + jnp.exp(-pre)) * acc[whole, unit:]).astype(BF16)
        for r in (2, 1, 3, 0):
            parts[k, r, whole, :] = jnp.dot(
                hidden, w_dn[r], preferred_element_type=F32
            ).astype(BF16)
            co["p", r] = send(parts.at[k, r, whole, THEIRS], crecv.at[k, r, whole], core)

    def chip_sum(k, r, rows_of):
        return parts[k, r, rows_of, :feat].astype(F32) + crecv[k, r, rows_of].astype(F32)

    def b_sum(k, r):
        if WIDE_OUT[k]:
            return chip_sum(k, r, B(k))
        return chip_sum(k, r, B(k)) + xb_in[k, r, A(k)].astype(F32)

    def e(k, r):
        wait(k, ("p", r))
        if not WIDE_OUT[k]:
            xb_out[k, r, A(k)] = chip_sum(k, r, NEAR_B(k)).astype(BF16)
            copies[k]["xb", r] = send(xb_out.at[k, r, A(k)], xb_in.at[k, r, A(k)], x_near)

    def wait_b(k, r):
        wait(k, ("p", r))
        if not WIDE_OUT[k]:
            wait(k, ("xb", r))

    def gC(k):
        wait(k, ("p", 2))
        rows_of = C_OUT(k)
        ring2[k, rows_of] = chip_sum(k, 2, rows_of).astype(BF16)
        device = y_two if STRAIGHT_OUT[k] else y_dn if up_AB(k) else y_up
        copies[k]["gC"] = send(ring2.at[k, rows_of], ring2_in.at[k, rows_of], device)

    def gAB(k):
        wait_b(k, 2)
        ring2[k, A(k)] = chip_sum(k, 2, A(k)).astype(BF16)
        ring2[k, B(k)] = b_sum(k, 2).astype(BF16)
        device = y_two if STRAIGHT_OUT[k] else y_up if up_AB(k) else y_dn
        copies[k]["gAB"] = send(ring2.at[k, AB(k)], ring2_in.at[k, AB(k)], device)

    def way(k, up):
        return (1, ring_up, ring_up_in, y_up) if up else (3, ring_dn, ring_dn_in, y_dn)

    def passing(k, name, rows_of):
        if STRAIGHT_OUT[k]:
            return 0.0
        wait(k, name)
        return ring2_in[k, rows_of].astype(F32)

    def sC1(k):
        r, buf, into, device = way(k, up_AB(k))
        wait(k, ("p", r))
        rows_of = C_OUT(k)
        buf[k, rows_of] = chip_sum(k, r, rows_of).astype(BF16)
        copies[k]["s1C"] = send(buf.at[k, rows_of], into.at[k, rows_of], device)

    def sAB1(k):
        r, buf, into, device = way(k, not up_AB(k))
        wait_b(k, r)
        buf[k, A(k)] = chip_sum(k, r, A(k)).astype(BF16)
        buf[k, B(k)] = b_sum(k, r).astype(BF16)
        copies[k]["s1AB"] = send(buf.at[k, AB(k)], into.at[k, AB(k)], device)

    def sAB2(k):
        r, buf, into, device = way(k, up_AB(k))
        wait_b(k, r)
        buf[k, A(k)] = (chip_sum(k, r, A(k)) + passing(k, "gAB", A(k))).astype(BF16)
        buf[k, B(k)] = (b_sum(k, r) + passing(k, "gAB", B(k))).astype(BF16)
        copies[k]["s2AB"] = send(buf.at[k, AB(k)], into.at[k, AB(k)], device)

    def sC2(k):
        r, buf, into, device = way(k, not up_AB(k))
        wait(k, ("p", r))
        rows_of = C_OUT(k)
        buf[k, rows_of] = (chip_sum(k, r, rows_of) + passing(k, "gC", rows_of)).astype(BF16)
        copies[k]["s2C"] = send(buf.at[k, rows_of], into.at[k, rows_of], device)

    def neighbours(k, rows_of):
        both = ring_up_in[k, rows_of].astype(F32) + ring_dn_in[k, rows_of].astype(F32)
        if STRAIGHT_OUT[k]:
            both = both + ring2_in[k, rows_of].astype(F32)
        return both

    def rC(k):
        wait(k, ("p", 0), "s1C", "s2C")
        if STRAIGHT_OUT[k]:
            wait(k, "gC")
        rows_of = C_OUT(k)
        into = AB(k) if WIDE_OUT[k] else A(k)
        xn_out[k, into] = (chip_sum(k, 0, rows_of) + neighbours(k, rows_of)).astype(BF16)
        copies[k]["xnback"] = send(xn_out.at[k, into], xn_in.at[k, into], x_near)

    def rAB(k):
        pair, lo, hi = CHUNKS[k]
        wait_b(k, 0)
        wait(k, "s1AB", "s2AB")
        if STRAIGHT_OUT[k]:
            wait(k, "gAB")
        crossing = b_sum(k, 0) + neighbours(k, B(k))
        if WIDE_OUT[k]:
            wait(k, "xnback")
            crossing = crossing + xn_in[k, B(k)].astype(F32)
        fin_x[pair, lo:hi] = crossing
        own[k, A(k)] = chip_sum(k, 0, A(k)) + neighbours(k, A(k))
        for j, first, last in ended(k):
            ret_x[j] = tall_block(fin_x[pair, first:last])
            to = ("z", at((z + j) % nz, nx - 1 - x, y, c)) if j else x_cross
            z_back.append(send(ret_x.at[j], retr.at[j, pl.ds(tall, tall)], to))

    def tall_block(block):
        return jnp.concatenate([block, jnp.zeros((tall - cap, feat), F32)], axis=0).astype(BF16)

    def ended(k):
        pair, lo, hi = CHUNKS[k]
        units = [(j, i * cap, (i + 1) * cap) for i, j in enumerate(PAIRS[pair])]
        return [unit for unit in units if lo < unit[2] <= hi]

    def r4(k):
        pair, lo, hi = CHUNKS[k]
        wait(k, "xnback")
        fin[pair, lo:hi] = own[k, A(k)] + xn_in[k, A(k)].astype(F32)
        for j, first, last in ended(k):
            block = tall_block(fin[pair, first:last])
            if j:
                ret_own[j] = block
                to = ("z", at((z + j) % nz, x, y, c))
                z_back.append(send(ret_own.at[j], retr.at[j, pl.ds(0, tall)], to))
            else:
                retr[0, :tall] = block

    z_back = []
    STAGES = dict(
        d1=d1, d2=d2, d3=d3, d4u=d4u, d4d=d4d, d4a=d4a, d5=d5, d6=d6, c=compute, e=e, gC=gC, gAB=gAB,
        sC1=sC1, sAB1=sAB1, sAB2=sAB2, sC2=sC2, rC=rC, rAB=rAB, r4=r4,
    )
    for name, *where in ORDER:
        STAGES[name](*where)

    for flight in z_back:
        finish(flight)
    back = retr[...].reshape(nz * 2 * tall, feat)
    merged = jnp.dot(slots_t[...], back, preferred_element_type=F32)
    out[...] = merged.astype(BF16)


def on_device(nx, ny, nz, tokens, routes, router_gate, w_gate, w_up, w_down):
    rows, feat = tokens.shape
    unit = w_gate.shape[1]
    cap = 3 * rows // (nx * nz)
    half, piece, tall = 4 * cap, 2 * cap, -(-cap // 16) * 16
    vm = pltpu.VMEM
    scratch = [
        vm((ny, 2 * feat, 2 * unit), BF16),
        vm((ny, unit, 2 * feat), BF16),
        vm((nz, 2 * cap, feat), BF16),
        vm((nz, 2 * cap, feat), BF16),
        vm((NC, piece, feat), BF16),
        vm((NC, ny, 2 * half, 2 * feat), BF16),
        vm((2 * half, 2 * unit), F32),
        vm((NC, ny, 2 * half, 2 * feat), BF16),
        vm((NC, ny, 2 * half, feat), BF16),
        vm((NC, ny, piece, feat), BF16),
        vm((NC, ny, piece, feat), BF16),
    ]
    scratch += [vm((NC, 2 * half, feat), BF16)] * 6
    scratch += [
        vm((NC, piece, feat), F32),
        vm((NC, half, feat), BF16),
        vm((NC, half, feat), BF16),
        vm((len(PAIRS), piece, feat), F32),
        vm((len(PAIRS), piece, feat), F32),
        vm((nz, tall, feat), BF16),
        vm((nz, tall, feat), BF16),
        vm((nz, 2 * tall, feat), BF16),
        vm((rows, feat), BF16),
        vm((rows, nz * 2 * tall), BF16),
        pltpu.SemaphoreType.DMA,
        pltpu.SemaphoreType.DMA((2,)),
        pltpu.SemaphoreType.DMA((SEMS[0],)),
        pltpu.SemaphoreType.DMA((SEMS[1],)),
    ]
    in_vmem = pl.BlockSpec(memory_space=pltpu.VMEM)
    in_hbm = pl.BlockSpec(memory_space=pl.ANY)
    return pl.pallas_call(
        functools.partial(kernel, (nx, ny, nz, cap, feat)),
        out_shape=jax.ShapeDtypeStruct((rows, feat), BF16),
        in_specs=[in_hbm] + [in_vmem] * 2 + [in_hbm] * 3,
        out_specs=in_vmem,
        scratch_shapes=scratch,
        compiler_params=pltpu.CompilerParams(
            collective_id=0, has_side_effects=True, vmem_limit_bytes=60 * 1024 * 1024
        ),
    )(tokens, routes.reshape(1, rows), router_gate.reshape(1, rows), w_gate, w_up, w_down)


def solution(mesh):
    nx, ny = 4, mesh.shape["etp"] // 2
    nz = mesh.shape["ep"] // nx
    return jax.shard_map(
        functools.partial(on_device, nx, ny, nz),
        mesh=mesh,
        in_specs=(
            P("ep", "etp"),
            P("ep", None),
            P("ep", None),
            P(None, ("ep", "etp")),
            P(None, ("ep", "etp")),
            P(("ep", "etp"), None),
        ),
        out_specs=P("ep", "etp"),
        check_vma=False,
    )
```

```python
import functools

import jax
import jax.numpy as jnp
from jax import lax
from jax.experimental import pallas as pl
from jax.experimental.pallas import tpu as pltpu
from jax.sharding import PartitionSpec as P

MESH = pl.DeviceIdType.MESH
F32 = jnp.float32
BF16 = jnp.bfloat16

PAIRS = ((0, 1), (6, 3), (5, 4), (7, 2))
CHUNKS = (
    (0, 0, 16),
    (0, 16, 48),
    (1, 0, 48),
    (2, 0, 32),
    (2, 32, 48),
    (3, 0, 32),
    (3, 32, 48),
)
WIDE_IN = (0, 0, 0, 0, 0, 0, 0)
WIDE_OUT = (0, 0, 0, 0, 0, 1, 0)
STRAIGHT_IN = (0, 0, 0, 0, 0, 0, 0)
STRAIGHT_OUT = (0, 0, 0, 0, 0, 0, 0)
FLIP = (0, 1, 0, 1, 0, 1, 0)
NC = len(CHUNKS)
SEMS = (52, 106)
Z_ORDER = (1, 7, 6, 2, 3, 5, 4)


ORDER = (
    ("d1", 0), ("d2", 0), ("d3", 0), ("d1", 1), ("d6", 0, 0), ("d4d", 0), ("d4u", 0), ("d4a", 0),
    ("d2", 1), ("d3", 1), ("d1", 5), ("d5", 0), ("d1", 6), ("d4d", 1), ("d2", 5), ("d4u", 1),
    ("d3", 5), ("d2", 6), ("d6", 1, 0), ("d4a", 1), ("d3", 6), ("d6", 0, 3), ("d1", 2), ("d4u", 5),
    ("d4u", 6), ("d6", 6, 0), ("d4d", 5), ("d6", 1, 3), ("d6", 0, 2), ("d6", 0, 1), ("d4a", 5),
    ("d6", 1, 1), ("d5", 1), ("d4a", 6), ("d2", 2), ("d3", 2), ("d1", 3), ("d1", 4), ("ca", 0),
    ("d6", 5, 3), ("d6", 5, 1), ("ca", 1), ("d5", 5), ("d6", 1, 2), ("d4d", 6), ("d5", 6),
    ("d6", 5, 0), ("d6", 6, 3), ("d4u", 2), ("d2", 3), ("c", 1), ("d4d", 2), ("d4a", 2), ("d2", 4),
    ("d3", 3), ("e", 1, 1), ("d6", 5, 2), ("d3", 4), ("ca", 5), ("gC", 1), ("d6", 6, 2),
    ("d6", 2, 0), ("d6", 6, 1), ("c", 5), ("d4d", 3), ("ca", 6), ("gC", 5), ("gAB", 5), ("d5", 2),
    ("d4d", 4), ("d6", 2, 3), ("c", 6), ("d6", 2, 1), ("d4u", 3), ("d4a", 3), ("d6", 3, 0),
    ("d4u", 4), ("e", 1, 2), ("gC", 6), ("e", 6, 2), ("sC1", 5), ("sAB1", 5), ("ca", 2),
    ("d6", 2, 2), ("e", 6, 1), ("d4a", 4), ("sC1", 1), ("e", 6, 3), ("d6", 3, 1), ("sC1", 6),
    ("c", 2), ("d5", 3), ("sC2", 6), ("sC2", 5), ("sAB2", 5), ("d6", 4, 1), ("d6", 3, 3),
    ("e", 2, 2), ("c", 0), ("gAB", 6), ("d5", 4), ("gC", 2), ("gAB", 1), ("e", 2, 3), ("sC1", 2),
    ("e", 2, 1), ("ca", 3), ("d6", 4, 3), ("sAB1", 6), ("d6", 3, 2), ("d6", 4, 0), ("rC", 5),
    ("gAB", 2), ("d6", 4, 2), ("c", 3), ("rC", 6), ("sC2", 1), ("sC2", 2), ("sAB1", 2), ("sAB2", 6),
    ("e", 3, 2), ("e", 6, 0), ("e", 2, 0), ("ca", 4), ("gC", 3), ("c", 4), ("sAB2", 2), ("e", 4, 2),
    ("e", 3, 1), ("e", 4, 3), ("rAB", 5), ("gC", 4), ("gAB", 3), ("rAB", 6), ("sC1", 3),
    ("e", 3, 3), ("e", 4, 1), ("r4", 5), ("r4", 6), ("rC", 2), ("sC1", 4), ("gAB", 4), ("e", 0, 2),
    ("e", 1, 3), ("e", 3, 0), ("gC", 0), ("sC2", 4), ("sC2", 3), ("e", 0, 1), ("sAB1", 4),
    ("sAB1", 3), ("e", 4, 0), ("rAB", 2), ("sAB2", 3), ("e", 0, 3), ("sAB2", 4), ("rC", 3),
    ("sC2", 0), ("gAB", 0), ("r4", 2), ("sC1", 0), ("sAB2", 1), ("rC", 4), ("e", 0, 0), ("sAB1", 1),
    ("e", 1, 0), ("rAB", 3), ("rAB", 4), ("rC", 1), ("sAB1", 0), ("sAB2", 0), ("rC", 0), ("r4", 3),
    ("r4", 4), ("rAB", 0), ("rAB", 1), ("r4", 0), ("r4", 1),
)

BACK = {"up": "dn", "dn": "up", "two": "two", "core": "core", "near": "near", "cross": "cross"}


def kernel(sizes, tokens, routes, gate, w_gate, w_up, w_down, out,
           w_gu, w_dn, outgo, zrecv, cross, xs, acc, parts, crecv, xb_out, xb_in,
           ring2, ring2_in, ring_up, ring_up_in, ring_dn, ring_dn_in,
           own, xn_out, xn_in, fin, fin_x, ret_own, ret_x, retr, tok, slots_t,
           t_sem, w_sem, send_sem, recv_sem):
    nx, ny, nz, cap, feat = sizes
    tall = -(-cap // 16) * 16
    ep = lax.axis_index("ep")
    etp = lax.axis_index("etp")
    z, x = ep // nx, ep % nx
    y, c = etp // 2, etp % 2

    def at(zz, xx, yy, cc):
        return {"ep": zz * nx + xx, "etp": yy * 2 + cc}

    y_up, y_dn = ("up", at(z, x, (y + 1) % ny, c)), ("dn", at(z, x, (y + ny - 1) % ny, c))
    y_two = ("two", at(z, x, (y + 2) % ny, c))
    core = ("core", at(z, x, y, 1 - c))
    x_near = ("near", at(z, x + 1 - 2 * (x % 2), y, c))
    x_cross = ("cross", at(z, nx - 1 - x, y, c))

    load_tokens = pltpu.make_async_copy(tokens, tok, t_sem)
    load_tokens.start()
    barrier = pltpu.get_barrier_semaphore()
    peers = [to[1] for to in (y_up, y_dn, core, x_near, x_cross)]
    if any(STRAIGHT_IN + STRAIGHT_OUT):
        peers.append(y_two[1])
    peers += [at((z + j) % nz, xx, y, c) for j in range(1, nz) for xx in (x, nx - 1 - x)]
    for peer in peers:
        pl.semaphore_signal(barrier, inc=1, device_id=peer, device_id_type=MESH)

    rows = routes.shape[1]
    expert = routes[...]
    onehot = (expert == lax.broadcasted_iota(jnp.int32, (nz * nx // 2, rows), 0)).astype(F32)
    before = lax.broadcasted_iota(jnp.int32, (rows, rows), 0) < lax.broadcasted_iota(
        jnp.int32, (rows, rows), 1
    )
    ranks = jnp.dot(onehot.astype(BF16), before.astype(F32).astype(BF16), preferred_element_type=F32)
    rank = jnp.sum(ranks * onehot, axis=0, keepdims=True).astype(jnp.int32)
    unit_of = (z + nz - (expert >> 1)) & (nz - 1)
    other = (expert & 1) != x // 2
    slot = unit_of * (2 * cap) + jnp.where(other, cap, 0) + rank
    place = lax.broadcasted_iota(jnp.int32, (nz * 2 * cap, rows), 0)
    chosen = (slot == place).astype(F32)
    load_tokens.wait()
    sent = jnp.dot(chosen.astype(BF16), tok[...], preferred_element_type=F32)
    outgo[...] = sent.astype(BF16).reshape(nz, 2 * cap, feat)
    clock, used = [0], [0, 0]
    heard = dict.fromkeys(BACK, -1)
    free_send, free_recv = [], []

    def send(src, dst, to):
        link, device = to
        clock[0] += 1
        if free_send:
            i = free_send.pop()
        else:
            i = used[0]
            used[0] += 1
        ready = [at_ for at_ in free_recv if link in BACK and at_[0] < heard[BACK[link]]]
        if ready:
            free_recv.remove(ready[0])
            j = ready[0][1]
        else:
            j = used[1]
            used[1] += 1
        copy = pltpu.make_async_remote_copy(
            src_ref=src, dst_ref=dst, send_sem=send_sem.at[i], recv_sem=recv_sem.at[j],
            device_id=device, device_id_type=MESH,
        )
        copy.start()
        return copy, link, clock[0], i, j

    def finish(flight):
        copy, link, sent_at, i, j = flight
        copy.wait_recv()
        copy.wait_send()
        clock[0] += 1
        if link in BACK:
            heard[link] = max(heard[link], sent_at)
        free_send.append(i)
        free_recv.append((clock[0], j))

    pl.semaphore_wait(barrier, len(peers))

    z_copy = {}
    for j in Z_ORDER:
        z_copy[j] = send(outgo.at[j], zrecv.at[j], ("z", at((z + nz - j) % nz, x, y, c)))

    unit = w_gate.shape[1]
    for r in range(ny):
        for k in range(2):
            shard = pl.ds(pl.multiple_of((((y + r) % ny) * 2 + (c + k) % 2) * feat, 128), feat)
            into = pl.ds(k * feat, feat)
            for source, target, sem in (
                (w_gate.at[shard, :], w_gu.at[r, into, pl.ds(0, unit)], 0),
                (w_up.at[shard, :], w_gu.at[r, into, pl.ds(unit, unit)], 0),
                (w_down.at[:, shard], w_dn.at[r, :, into], 1),
            ):
                pltpu.make_async_copy(source, target, w_sem.at[sem]).start()
    loads = [pltpu.make_async_copy(w, w, w_sem.at[i]) for i, w in enumerate((w_gu, w_dn))]

    back_slot = unit_of * (2 * tall) + jnp.where(other, tall, 0) + rank
    back_place = lax.broadcasted_iota(jnp.int32, (nz * 2 * tall, rows), 0)
    weighted = jnp.where(back_slot == back_place, gate[...].astype(F32), 0.0)
    slots_t[...] = weighted.T.astype(BF16)

    MINE, THEIRS = pl.ds(0, feat), pl.ds(feat, feat)
    n_of = [hi - lo for _, lo, hi in CHUNKS]

    def A(k):
        return pl.ds(0, n_of[k])

    def B(k):
        return pl.ds(n_of[k], n_of[k])

    def AB(k):
        return pl.ds(0, 2 * n_of[k])

    def ALL(k):
        return pl.ds(0, 4 * n_of[k])

    def NEAR_A(k):
        return pl.ds(2 * n_of[k], n_of[k])

    def NEAR_B(k):
        return pl.ds(3 * n_of[k], n_of[k])

    def C_IN(k):
        return pl.ds(2 * n_of[k], (2 if WIDE_IN[k] else 1) * n_of[k])

    def C_OUT(k):
        return pl.ds(2 * n_of[k], (2 if WIDE_OUT[k] else 1) * n_of[k])

    copies = [dict() for _ in CHUNKS]

    def wait(k, *names):
        for name in names:
            flight = copies[k][name]
            if flight is not None:
                finish(flight)
                copies[k][name] = None

    def take(k, off):
        pair, lo, hi = CHUNKS[k]
        found = []
        for i, j in enumerate(PAIRS[pair]):
            first, last = max(lo - i * cap, 0), min(hi - i * cap, cap)
            if first < last:
                if j in z_copy:
                    finish(z_copy.pop(j))
                block = (zrecv if j else outgo)[j].astype(F32)
                found.append(block[off + first : off + last])
        return jnp.concatenate(found, axis=0).astype(BF16) if len(found) > 1 else found[0].astype(BF16)

    def d1(k):
        co = copies[k]
        cross[k, A(k)] = take(k, cap)
        co["cross"] = send(cross.at[k, A(k)], xs.at[k, 0, B(k), MINE], x_cross)
        xs[k, 0, A(k), :feat] = take(k, 0)
        mine = xs.at[k, 0, A(k), MINE]
        co["xnA"] = send(mine, xs.at[k, 0, NEAR_A(k), MINE], x_near)
        co["upA"] = send(mine, xs.at[k, 3, A(k), MINE], y_up)
        co["dnA"] = send(mine, xs.at[k, 1, A(k), MINE], y_dn)
        if STRAIGHT_IN[k]:
            co["y2A"] = send(mine, xs.at[k, 2, A(k), MINE], y_two)

    def near_b(k, r):
        copies[k]["xnB", r] = send(xs.at[k, r, B(k), MINE], xs.at[k, r, NEAR_B(k), MINE], x_near)

    def d2(k):
        co = copies[k]
        wait(k, "cross")
        near_b(k, 0)
        mine = xs.at[k, 0, B(k), MINE]
        co["upB"] = send(mine, xs.at[k, 3, B(k), MINE], y_up)
        co["dnB"] = send(mine, xs.at[k, 1, B(k), MINE], y_dn)
        if STRAIGHT_IN[k]:
            co["y2B"] = send(mine, xs.at[k, 2, B(k), MINE], y_two)
        co["c0"] = send(xs.at[k, 0, AB(k), MINE], xs.at[k, 0, AB(k), THEIRS], core)

    def d3(k):
        co = copies[k]
        wait(k, "xnA")
        if WIDE_IN[k]:
            wait(k, ("xnB", 0))
        rows_c = C_IN(k)
        mine = xs.at[k, 0, rows_c, MINE]
        co["upC"] = send(mine, xs.at[k, 3, rows_c, MINE], y_up)
        co["dnC"] = send(mine, xs.at[k, 1, rows_c, MINE], y_dn)
        if STRAIGHT_IN[k]:
            co["y2C"] = send(mine, xs.at[k, 2, rows_c, MINE], y_two)
        co["c0C"] = send(mine, xs.at[k, 0, rows_c, THEIRS], core)

    def pass_on(k, up, rows_of):
        src, device = (3, y_up) if up else (1, y_dn)
        return send(xs.at[k, src, rows_of, MINE], xs.at[k, 2, rows_of, MINE], device)

    def up_AB(k):
        return not FLIP[k]

    def d4u(k):
        wait(k, "upA", "upB")
        if not WIDE_IN[k]:
            near_b(k, 3)
        if up_AB(k) and not STRAIGHT_IN[k]:
            copies[k]["fAB"] = pass_on(k, True, AB(k))

    def d4d(k):
        wait(k, "dnA", "dnB")
        if not WIDE_IN[k]:
            near_b(k, 1)
        if not up_AB(k) and not STRAIGHT_IN[k]:
            copies[k]["fAB"] = pass_on(k, False, AB(k))

    def to_core(k, r):
        rows_of = pl.ds(0, (4 if WIDE_IN[k] else 3) * n_of[k])
        copies[k]["c", r] = send(xs.at[k, r, rows_of, MINE], xs.at[k, r, rows_of, THEIRS], core)

    def d4a(k):
        wait(k, "upA", "upB", "dnA", "dnB", "upC", "dnC")
        if not STRAIGHT_IN[k]:
            copies[k]["fC"] = pass_on(k, not up_AB(k), C_IN(k))
        to_core(k, 1)
        to_core(k, 3)

    def d5(k):
        wait(k, *(("y2A", "y2B", "y2C") if STRAIGHT_IN[k] else ("fAB", "fC")))
        if not WIDE_IN[k]:
            near_b(k, 2)
        to_core(k, 2)

    def d6(k, r):
        if not WIDE_IN[k]:
            wait(k, ("xnB", r))
            mine = xs.at[k, r, NEAR_B(k), MINE]
            copies[k]["cB", r] = send(mine, xs.at[k, r, NEAR_B(k), THEIRS], core)

    def gate_up(k, r):
        if r == 0:
            wait(k, "c0", "c0C")
        else:
            wait(k, ("c", r))
        if not WIDE_IN[k]:
            wait(k, ("cB", r))
        return jnp.dot(xs[k, r, ALL(k), :], w_gu[r], preferred_element_type=F32)

    def early(k):
        while loads:
            loads.pop().wait()
        acc[k, ALL(k), :] = gate_up(k, 0)
        for r in (1, 3):
            acc[k, ALL(k), :] += gate_up(k, r)

    def compute(k):
        co = copies[k]
        whole = ALL(k)
        both = acc[k, whole, :] + gate_up(k, 2)
        unit = w_gate.shape[1]
        pre = both[:, :unit]
        hidden = (pre / (1.0 + jnp.exp(-pre)) * both[:, unit:]).astype(BF16)
        for r in (2, 1, 3, 0):
            parts[k, r, whole, :] = jnp.dot(
                hidden, w_dn[r], preferred_element_type=F32
            ).astype(BF16)
            co["p", r] = send(parts.at[k, r, whole, THEIRS], crecv.at[k, r, whole], core)

    def chip_sum(k, r, rows_of):
        return parts[k, r, rows_of, :feat].astype(F32) + crecv[k, r, rows_of].astype(F32)

    def b_sum(k, r):
        if WIDE_OUT[k]:
            return chip_sum(k, r, B(k))
        return chip_sum(k, r, B(k)) + xb_in[k, r, A(k)].astype(F32)

    def e(k, r):
        wait(k, ("p", r))
        if not WIDE_OUT[k]:
            xb_out[k, r, A(k)] = chip_sum(k, r, NEAR_B(k)).astype(BF16)
            copies[k]["xb", r] = send(xb_out.at[k, r, A(k)], xb_in.at[k, r, A(k)], x_near)

    def wait_b(k, r):
        wait(k, ("p", r))
        if not WIDE_OUT[k]:
            wait(k, ("xb", r))

    def gC(k):
        wait(k, ("p", 2))
        rows_of = C_OUT(k)
        ring2[k, rows_of] = chip_sum(k, 2, rows_of).astype(BF16)
        device = y_two if STRAIGHT_OUT[k] else y_dn if up_AB(k) else y_up
        copies[k]["gC"] = send(ring2.at[k, rows_of], ring2_in.at[k, rows_of], device)

    def gAB(k):
        wait_b(k, 2)
        ring2[k, A(k)] = chip_sum(k, 2, A(k)).astype(BF16)
        ring2[k, B(k)] = b_sum(k, 2).astype(BF16)
        device = y_two if STRAIGHT_OUT[k] else y_up if up_AB(k) else y_dn
        copies[k]["gAB"] = send(ring2.at[k, AB(k)], ring2_in.at[k, AB(k)], device)

    def way(k, up):
        return (1, ring_up, ring_up_in, y_up) if up else (3, ring_dn, ring_dn_in, y_dn)

    def passing(k, name, rows_of):
        if STRAIGHT_OUT[k]:
            return 0.0
        wait(k, name)
        return ring2_in[k, rows_of].astype(F32)

    def sC1(k):
        r, buf, into, device = way(k, up_AB(k))
        wait(k, ("p", r))
        rows_of = C_OUT(k)
        buf[k, rows_of] = chip_sum(k, r, rows_of).astype(BF16)
        copies[k]["s1C"] = send(buf.at[k, rows_of], into.at[k, rows_of], device)

    def sAB1(k):
        r, buf, into, device = way(k, not up_AB(k))
        wait_b(k, r)
        buf[k, A(k)] = chip_sum(k, r, A(k)).astype(BF16)
        buf[k, B(k)] = b_sum(k, r).astype(BF16)
        copies[k]["s1AB"] = send(buf.at[k, AB(k)], into.at[k, AB(k)], device)

    def sAB2(k):
        r, buf, into, device = way(k, up_AB(k))
        wait_b(k, r)
        buf[k, A(k)] = (chip_sum(k, r, A(k)) + passing(k, "gAB", A(k))).astype(BF16)
        buf[k, B(k)] = (b_sum(k, r) + passing(k, "gAB", B(k))).astype(BF16)
        copies[k]["s2AB"] = send(buf.at[k, AB(k)], into.at[k, AB(k)], device)

    def sC2(k):
        r, buf, into, device = way(k, not up_AB(k))
        wait(k, ("p", r))
        rows_of = C_OUT(k)
        buf[k, rows_of] = (chip_sum(k, r, rows_of) + passing(k, "gC", rows_of)).astype(BF16)
        copies[k]["s2C"] = send(buf.at[k, rows_of], into.at[k, rows_of], device)

    def neighbours(k, rows_of):
        both = ring_up_in[k, rows_of].astype(F32) + ring_dn_in[k, rows_of].astype(F32)
        if STRAIGHT_OUT[k]:
            both = both + ring2_in[k, rows_of].astype(F32)
        return both

    def rC(k):
        wait(k, ("p", 0), "s1C", "s2C")
        if STRAIGHT_OUT[k]:
            wait(k, "gC")
        rows_of = C_OUT(k)
        into = AB(k) if WIDE_OUT[k] else A(k)
        xn_out[k, into] = (chip_sum(k, 0, rows_of) + neighbours(k, rows_of)).astype(BF16)
        copies[k]["xnback"] = send(xn_out.at[k, into], xn_in.at[k, into], x_near)

    def rAB(k):
        pair, lo, hi = CHUNKS[k]
        wait_b(k, 0)
        wait(k, "s1AB", "s2AB")
        if STRAIGHT_OUT[k]:
            wait(k, "gAB")
        crossing = b_sum(k, 0) + neighbours(k, B(k))
        if WIDE_OUT[k]:
            wait(k, "xnback")
            crossing = crossing + xn_in[k, B(k)].astype(F32)
        fin_x[pair, lo:hi] = crossing
        own[k, A(k)] = chip_sum(k, 0, A(k)) + neighbours(k, A(k))
        for j, first, last in ended(k):
            ret_x[j] = tall_block(fin_x[pair, first:last])
            to = ("z", at((z + j) % nz, nx - 1 - x, y, c)) if j else x_cross
            z_back.append(send(ret_x.at[j], retr.at[j, pl.ds(tall, tall)], to))

    def tall_block(block):
        return jnp.concatenate([block, jnp.zeros((tall - cap, feat), F32)], axis=0).astype(BF16)

    def ended(k):
        pair, lo, hi = CHUNKS[k]
        units = [(j, i * cap, (i + 1) * cap) for i, j in enumerate(PAIRS[pair])]
        return [unit for unit in units if lo < unit[2] <= hi]

    def r4(k):
        pair, lo, hi = CHUNKS[k]
        wait(k, "xnback")
        fin[pair, lo:hi] = own[k, A(k)] + xn_in[k, A(k)].astype(F32)
        for j, first, last in ended(k):
            block = tall_block(fin[pair, first:last])
            if j:
                ret_own[j] = block
                to = ("z", at((z + j) % nz, x, y, c))
                z_back.append(send(ret_own.at[j], retr.at[j, pl.ds(0, tall)], to))
            else:
                retr[0, :tall] = block

    z_back = []
    STAGES = dict(
        d1=d1, d2=d2, d3=d3, d4u=d4u, d4d=d4d, d4a=d4a, d5=d5, d6=d6, ca=early, c=compute, e=e, gC=gC, gAB=gAB,
        sC1=sC1, sAB1=sAB1, sAB2=sAB2, sC2=sC2, rC=rC, rAB=rAB, r4=r4,
    )
    for name, *where in ORDER:
        STAGES[name](*where)

    for flight in z_back:
        finish(flight)
    back = retr[...].reshape(nz * 2 * tall, feat)
    merged = jnp.dot(slots_t[...], back, preferred_element_type=F32)
    out[...] = merged.astype(BF16)


def on_device(nx, ny, nz, tokens, routes, router_gate, w_gate, w_up, w_down):
    rows, feat = tokens.shape
    unit = w_gate.shape[1]
    cap = 3 * rows // (nx * nz)
    half, piece, tall = 4 * cap, 2 * cap, -(-cap // 16) * 16
    vm = pltpu.VMEM
    scratch = [
        vm((ny, 2 * feat, 2 * unit), BF16),
        vm((ny, unit, 2 * feat), BF16),
        vm((nz, 2 * cap, feat), BF16),
        vm((nz, 2 * cap, feat), BF16),
        vm((NC, piece, feat), BF16),
        vm((NC, ny, 2 * half, 2 * feat), BF16),
        vm((NC, 2 * half, 2 * unit), F32),
        vm((NC, ny, 2 * half, 2 * feat), BF16),
        vm((NC, ny, 2 * half, feat), BF16),
        vm((NC, ny, piece, feat), BF16),
        vm((NC, ny, piece, feat), BF16),
    ]
    scratch += [vm((NC, 2 * half, feat), BF16)] * 6
    scratch += [
        vm((NC, piece, feat), F32),
        vm((NC, half, feat), BF16),
        vm((NC, half, feat), BF16),
        vm((len(PAIRS), piece, feat), F32),
        vm((len(PAIRS), piece, feat), F32),
        vm((nz, tall, feat), BF16),
        vm((nz, tall, feat), BF16),
        vm((nz, 2 * tall, feat), BF16),
        vm((rows, feat), BF16),
        vm((rows, nz * 2 * tall), BF16),
        pltpu.SemaphoreType.DMA,
        pltpu.SemaphoreType.DMA((2,)),
        pltpu.SemaphoreType.DMA((SEMS[0],)),
        pltpu.SemaphoreType.DMA((SEMS[1],)),
    ]
    in_vmem = pl.BlockSpec(memory_space=pltpu.VMEM)
    in_hbm = pl.BlockSpec(memory_space=pl.ANY)
    return pl.pallas_call(
        functools.partial(kernel, (nx, ny, nz, cap, feat)),
        out_shape=jax.ShapeDtypeStruct((rows, feat), BF16),
        in_specs=[in_hbm] + [in_vmem] * 2 + [in_hbm] * 3,
        out_specs=in_vmem,
        scratch_shapes=scratch,
        compiler_params=pltpu.CompilerParams(
            collective_id=0, has_side_effects=True, vmem_limit_bytes=60 * 1024 * 1024
        ),
    )(tokens, routes.reshape(1, rows), router_gate.reshape(1, rows), w_gate, w_up, w_down)


def solution(mesh):
    nx, ny = 4, mesh.shape["etp"] // 2
    nz = mesh.shape["ep"] // nx
    return jax.shard_map(
        functools.partial(on_device, nx, ny, nz),
        mesh=mesh,
        in_specs=(
            P("ep", "etp"),
            P("ep", None),
            P("ep", None),
            P(None, ("ep", "etp")),
            P(None, ("ep", "etp")),
            P(("ep", "etp"), None),
        ),
        out_specs=P("ep", "etp"),
        check_vma=False,
    )
```
